256 devices in a mesh: grp: 8 (over y, core), mem: 32 (over x, z).
Axes of the slice: x: 4, y: 4, z: 8, core: 2. Of those that a mesh axis runs over, the one named last changes fastest.
Arguments:
- old_rows: bfloat16 [65536, 1024], P(('grp', 'mem')), may hold values from -24 to 24
- new_rows: bfloat16 [65536, 1024], P(('grp', 'mem')), may hold values from -6 to 6
- list_ids: int32 [65536], P(('grp', 'mem')), may hold values from 0 to 65535, as said below
- owner_map: int32 [65536], replicated, may hold values from 0 to 31, as said below
Outputs:
- owner_rows: float32 [131072, 1024], P(('grp', 'mem'))
- rotation: bfloat16 [1024, 1024], P('mem')
The draws below stay inside these ranges and needn't reach their ends.
Inputs may be any that keep to these rules, and one draw needn't show every extreme that they name: `list_ids`: in each device's block of 256 rows, at most 16 rows belong to lists of any one owner; in every group some owner receives exactly 16 rows from every device of the group. `owner_map`: every owner holds 65536 // 32 lists.
All inputs are finite; a program needn't handle non-finite values.
Results may differ from the reference program's by a relative error of at most 0.023.
Values may be sent and summed in bfloat16 or wider, within the bound.
No kernel may reach another device: no remote copies, remote signals or barrier semaphores. Data moves between devices by JAX's collectives and lax.ppermute only.
A program may use at most 64 MiB of HBM per device.

```python
import math
import jax
import jax.numpy as jnp
from jax import lax

D = 1024
LISTS = 65536
ROWS_DEV = 256
ITERS = 2
CAP = 16
SLOTS = 512
TOTAL_ROWS = 65536
N_GRP = 8
N_MEM = 32


def shared_lists(key):
    return jax.random.permutation(jax.random.fold_in(key, 11), LISTS).astype(jnp.int32)


def draw_owner_map(key, part):
    ordering = shared_lists(key)
    owners = (jnp.arange(LISTS, dtype=jnp.int32) % N_MEM).astype(jnp.int32)
    return jnp.zeros((LISTS,), jnp.int32).at[ordering].set(owners)


def draw_list_ids(key, part):
    ordering = shared_lists(key)
    busy_owner = jax.random.randint(jax.random.fold_in(key, 12), (N_GRP,), 0, N_MEM).astype(jnp.int32)
    device_keys = jax.random.split(jax.random.fold_in(key, 13), N_GRP * N_MEM)

    def draw_device(device_key, busy):
        pool_key = jax.random.fold_in(device_key, 1)
        order_key = jax.random.fold_in(device_key, 2)
        list_key = jax.random.fold_in(device_key, 3)
        slot_pool = jax.random.permutation(pool_key, (N_MEM - 1) * CAP).astype(jnp.int32)[:ROWS_DEV - CAP]
        others = slot_pool // CAP
        others = others + (others >= busy).astype(jnp.int32)
        owners = jnp.concatenate([jnp.full((CAP,), busy, jnp.int32), others.astype(jnp.int32)])
        owners = jax.random.permutation(order_key, owners).astype(jnp.int32)
        list_pick = jax.random.randint(list_key, (ROWS_DEV,), 0, LISTS // N_MEM).astype(jnp.int32)
        return ordering[owners + N_MEM * list_pick]
    busy_each = jnp.repeat(busy_owner, N_MEM)
    return jax.vmap(draw_device)(device_keys, busy_each).reshape(-1).astype(jnp.int32)


def spiked(drawn, rng, source, target, shards_of, factor):
    def block_of(dim):
        return (jnp.arange(drawn.shape[dim]) // (drawn.shape[dim] // shards_of)).reshape((-1,) + (1,) * (drawn.ndim - 1 - dim))

    first = jax.random.permutation(rng, shards_of)[block_of(target)]
    other_side = (block_of(target) + shards_of // 2) % shards_of
    return jnp.where((block_of(source) == first) | (block_of(source) == other_side), factor * drawn, drawn)


def block_levels(stream_key, extent, shards, smallest, high):
    def one(axis_at, shards_of):
        steps = jax.random.uniform(jax.random.fold_in(jax.random.fold_in(stream_key, 6), axis_at), (shards_of,), jnp.float32, smallest / len(shards), high / len(shards))
        return jnp.repeat(jnp.exp(steps), extent[axis_at] // shards_of).reshape((-1,) + (1,) * (len(extent) - axis_at - 1))

    factor_of = one(*shards[0])
    for cut in shards[1:]:
        factor_of = factor_of * one(*cut)
    return factor_of


def normal_values(own_key, extent, scale, most, cuts=(), kind=jnp.bfloat16):
    gain = block_levels(own_key, extent, cuts, -0.22, 0.18) if cuts else 1.0
    drawn = jax.random.normal(own_key, extent, jnp.float32) * scale * gain
    return jnp.minimum(jnp.maximum(drawn, -most), most).astype(kind)


def heavy_noise(key, dims, deviation, most, cuts, heavy, kind=jnp.bfloat16):
    values = deviation * jax.random.normal(key, dims, jnp.float32)
    if cuts:
        values = values * block_levels(key, dims, cuts, -0.22, 0.18)
    return jnp.clip(spiked(values, jax.random.fold_in(key, 3), *heavy), -most, most).astype(kind)


def setup_inputs(seed: int = 0) -> dict:
    seeds = jax.random.split(jax.random.key(seed), 5)
    return {
        "old_rows": heavy_noise(seeds[0], (TOTAL_ROWS, D), 1.0, 24.0, ((0, 256),), (0, 1, 256, 6.0)),
        "new_rows": normal_values(seeds[1], (TOTAL_ROWS, D), 1.0, 6.0, ((0, 256),)),
        "list_ids": draw_list_ids(jax.random.fold_in(seeds[4], 71), 0),
        "owner_map": draw_owner_map(jax.random.fold_in(seeds[4], 71), 0),
    }


EPSILON = 1e-06
COEFF_ONE = 3.4445
COEFF_THREE = -4.775
COEFF_FIVE = 2.0315

def polar_factor(covariance):
    squares = jnp.sum(covariance * covariance)
    iterate = (covariance * (0.25 * math.sqrt(D)) / jnp.sqrt(squares + EPSILON)).astype(jnp.bfloat16)
    for sweep in range(ITERS):
        gram = jnp.dot(iterate, iterate.T, preferred_element_type=jnp.float32).astype(jnp.bfloat16)
        first = jnp.dot(gram, iterate, preferred_element_type=jnp.float32).astype(jnp.bfloat16)
        second = jnp.dot(gram, first, preferred_element_type=jnp.float32)
        iterate = (COEFF_ONE * iterate.astype(jnp.float32) + COEFF_THREE * first.astype(jnp.float32) + COEFF_FIVE * second).astype(jnp.bfloat16)
    return iterate

def reference(old_rows, new_rows, list_ids, owner_map):
    covariance = jnp.dot(old_rows.T, new_rows, preferred_element_type=jnp.float32)
    rotation = polar_factor(covariance)
    rotated = jnp.dot(old_rows, rotation, preferred_element_type=jnp.float32)
    devices_all = N_GRP * N_MEM
    owner_of_row = owner_map[list_ids].astype(jnp.int32)
    onehot = (owner_of_row.reshape(devices_all, ROWS_DEV, 1) == jnp.arange(N_MEM, dtype=jnp.int32)).astype(jnp.int32)
    earlier = jnp.cumsum(onehot, axis=1) - onehot
    slot_index = lax.optimization_barrier(jnp.sum(earlier * onehot, axis=2)).reshape(-1).astype(jnp.int32)
    device = (jnp.arange(TOTAL_ROWS, dtype=jnp.int32) // ROWS_DEV).astype(jnp.int32)
    group_of = device // N_MEM
    source = device % N_MEM
    target = ((group_of * N_MEM + owner_of_row) * N_MEM + source) * CAP + slot_index
    owner_rows = jnp.zeros((N_GRP * N_MEM * SLOTS, D), jnp.float32).at[target].set(rotated)
    return (owner_rows, rotation)
```

```python
import math

import jax
import jax.numpy as jnp
from jax import lax
from jax.sharding import Mesh
from jax.sharding import PartitionSpec as P

ITERS = 2

EPSILON = 1e-06
COEFF_ONE = 3.4445
COEFF_THREE = -4.775
COEFF_FIVE = 2.0315

ALL = ("y", "core", "x", "z")
MEM = ("x", "z")
F32 = jnp.float32
BF16 = jnp.bfloat16


def dot(a, b):
    return jnp.dot(a, b, preferred_element_type=F32)


def swap_core(value):
    return lax.ppermute(value, "core", [(0, 1), (1, 0)])


def exchange(value, axes):
    return lax.all_to_all(value, axes, split_axis=0, concat_axis=0, tiled=True)


def outgoing_rows(old_rows, list_ids, owner_map, members):
    row_total = old_rows.shape[0]
    capacity = 2 * row_total // members
    owner = owner_map[list_ids]
    index = jnp.arange(row_total, dtype=jnp.int32)
    earlier = (owner[:, None] == owner[None, :]) & (index[None, :] < index[:, None])
    target = owner * capacity + jnp.sum(earlier.astype(jnp.int32), axis=1)
    slots = jnp.arange(members * capacity, dtype=jnp.int32)
    place = (slots[:, None] == target[None, :]).astype(BF16)
    return dot(place, old_rows).astype(BF16)


def covariance_of(old_rows, new_rows):
    features = old_rows.shape[1]
    half = features // 2
    core = lax.axis_index("core")
    mine = lax.dynamic_slice_in_dim(new_rows, core * half, half, 1)
    theirs = lax.dynamic_slice_in_dim(new_rows, (1 - core) * half, half, 1)
    old_pair = swap_core(old_rows)
    new_pair = swap_core(theirs)
    part = (dot(old_rows.T, mine) + dot(old_pair.T, new_pair)).astype(BF16)
    planes = lax.axis_size("y") * lax.axis_size("x")
    block = features // planes
    arrived = exchange(part, ("y", "x")).reshape(planes, block, half)
    part = jnp.sum(arrived.astype(F32), axis=0).astype(BF16)
    depth = lax.axis_size("z")
    copies = jnp.broadcast_to(part[None], (depth, block, half))
    arrived = exchange(copies, "z")
    total = jnp.sum(arrived.astype(F32), axis=0).astype(BF16)
    copies = jnp.broadcast_to(total[None], (planes, block, half))
    own_half = exchange(copies, ("y", "x")).reshape(features, half)
    other_half = swap_core(own_half)
    low = jnp.where(core == 0, own_half, other_half)
    high = jnp.where(core == 0, other_half, own_half)
    return jnp.concatenate([low, high], axis=1)


def local(old_rows, new_rows, list_ids, owner_map):
    features = old_rows.shape[1]
    members = lax.axis_size(MEM)
    block_rows = features // members
    scaling = 0.25 * math.sqrt(features)
    sent = outgoing_rows(old_rows, list_ids, owner_map, members)
    received = exchange(sent, MEM)
    covariance = covariance_of(old_rows, new_rows).astype(F32)
    squares = jnp.sum(covariance * covariance)
    iterate = (covariance * scaling / jnp.sqrt(squares + EPSILON)).astype(BF16)
    for sweep in range(ITERS):
        gram = dot(iterate, iterate.T).astype(BF16)
        first = dot(gram, iterate).astype(BF16)
        second = dot(gram, first)
        iterate = (
            COEFF_ONE * iterate.astype(F32) + COEFF_THREE * first.astype(F32) + COEFF_FIVE * second
        ).astype(BF16)
    own_rows = lax.dynamic_slice_in_dim(iterate, lax.axis_index(MEM) * block_rows, block_rows, 0)
    return (dot(received, iterate), own_rows)


def solution(mesh):
    shape = mesh.shape
    grid = mesh.devices.reshape(shape["grp"] // 2, 2, 4, shape["mem"] // 4)
    fine = Mesh(grid, ALL)
    in_specs = (P(ALL, None), P(ALL, None), P(ALL), P())
    out_specs = (P(ALL, None), P(MEM, None))
    return jax.shard_map(local, mesh=fine, in_specs=in_specs, out_specs=out_specs, check_vma=False)
```

```python
import math

import jax
import jax.numpy as jnp
from jax import lax
from jax.sharding import Mesh
from jax.sharding import PartitionSpec as P

ITERS = 2

EPSILON = 1e-06
COEFF_ONE = 3.4445
COEFF_THREE = -4.775
COEFF_FIVE = 2.0315

ALL = ("y", "core", "x", "zh", "zl")
MEM = ("x", "zh", "zl")
SPREAD = ("y", "x", "zl")
F32 = jnp.float32
BF16 = jnp.bfloat16


def dot(a, b):
    return jnp.dot(a, b, preferred_element_type=F32)


def swap_core(value):
    return lax.ppermute(value, "core", [(0, 1), (1, 0)])


def exchange(value, axes):
    return lax.all_to_all(value, axes, split_axis=0, concat_axis=0, tiled=True)


def outgoing_rows(old_rows, list_ids, owner_map, members):
    row_total = old_rows.shape[0]
    capacity = 2 * row_total // members
    owner = owner_map[list_ids]
    index = jnp.arange(row_total, dtype=jnp.int32)
    earlier = (owner[:, None] == owner[None, :]) & (index[None, :] < index[:, None])
    target = owner * capacity + jnp.sum(earlier.astype(jnp.int32), axis=1)
    slots = jnp.arange(members * capacity, dtype=jnp.int32)
    place = (slots[:, None] == target[None, :]).astype(BF16)
    return dot(place, old_rows).astype(BF16)


def covariance_of(old_rows, new_rows):
    features = old_rows.shape[1]
    half = features // 2
    core = lax.axis_index("core")
    mine = lax.dynamic_slice_in_dim(new_rows, core * half, half, 1)
    theirs = lax.dynamic_slice_in_dim(new_rows, (1 - core) * half, half, 1)
    old_pair = swap_core(old_rows)
    new_pair = swap_core(theirs)
    part = (dot(old_rows.T, mine) + dot(old_pair.T, new_pair)).astype(BF16)
    planes = lax.axis_size(SPREAD)
    block = features // planes
    arrived = exchange(part, SPREAD).reshape(planes, block, half)
    part = jnp.sum(arrived.astype(F32), axis=0).astype(BF16)
    depth = lax.axis_size("zh")
    copies = jnp.broadcast_to(part[None], (depth, block, half))
    arrived = exchange(copies, "zh").reshape(depth, block, half)
    total = jnp.sum(arrived.astype(F32), axis=0).astype(BF16)
    width = lax.axis_size("y")
    copies = jnp.broadcast_to(total[None], (planes // width, block, half))
    slab = exchange(copies.reshape(features // width, half), ("x", "zl"))
    rows = features // width
    y = lax.axis_index("y")
    covariance = jnp.zeros((features, features), BF16)
    for shift in range(width):
        perm = [(i, (i + shift) % width) for i in range(width)]
        own = slab if shift == 0 else lax.ppermute(slab, "y", perm)
        other = swap_core(own)
        low = jnp.where(core == 0, own, other)
        high = jnp.where(core == 0, other, own)
        both = jnp.concatenate([low, high], axis=1)
        start = ((y - shift) % width) * rows
        covariance = lax.dynamic_update_slice_in_dim(covariance, both, start, 0)
    return covariance


def local(old_rows, new_rows, list_ids, owner_map):
    features = old_rows.shape[1]
    members = lax.axis_size(MEM)
    block_rows = features // members
    scaling = 0.25 * math.sqrt(features)
    sent = outgoing_rows(old_rows, list_ids, owner_map, members)
    received = exchange(sent, MEM)
    covariance = covariance_of(old_rows, new_rows).astype(F32)
    squares = jnp.sum(covariance * covariance)
    iterate = (covariance * scaling / jnp.sqrt(squares + EPSILON)).astype(BF16)
    for sweep in range(ITERS):
        gram = dot(iterate, iterate.T).astype(BF16)
        first = dot(gram, iterate).astype(BF16)
        second = dot(gram, first)
        iterate = (
            COEFF_ONE * iterate.astype(F32) + COEFF_THREE * first.astype(F32) + COEFF_FIVE * second
        ).astype(BF16)
    own_rows = lax.dynamic_slice_in_dim(iterate, lax.axis_index(MEM) * block_rows, block_rows, 0)
    return (dot(received, iterate), own_rows)


def solution(mesh):
    shape = mesh.shape
    grid = mesh.devices.reshape(shape["grp"] // 2, 2, 4, shape["mem"] // 8, 2)
    fine = Mesh(grid, ALL)
    in_specs = (P(ALL, None), P(ALL, None), P(ALL), P())
    out_specs = (P(ALL, None), P(MEM, None))
    return jax.shard_map(local, mesh=fine, in_specs=in_specs, out_specs=out_specs, check_vma=False)
```

```python
import math

import jax
import jax.numpy as jnp
from jax import lax
from jax.experimental import pallas as pl
from jax.experimental.pallas import tpu as pltpu
from jax.sharding import Mesh
from jax.sharding import PartitionSpec as P

WIDTH = 4

EPSILON = 1e-06
COEFF_ONE = 3.4445
COEFF_THREE = -4.775
COEFF_FIVE = 2.0315

ALL = ("y", "core", "x", "zh", "zl")
MEM = ("x", "zh", "zl")
SPREAD = ("y", "x", "zl")
F32 = jnp.float32
BF16 = jnp.bfloat16


def dot(a, b):
    return jnp.dot(a, b, preferred_element_type=F32)


def swap_core(value):
    return lax.ppermute(value, "core", [(0, 1), (1, 0)])


def exchange(value, axes):
    return lax.all_to_all(value, axes, split_axis=0, concat_axis=0, tiled=True)


def outgoing_rows(old_rows, list_ids, owner_map, members):
    row_total = old_rows.shape[0]
    capacity = 2 * row_total // members
    owner = owner_map[list_ids]
    index = jnp.arange(row_total, dtype=jnp.int32)
    earlier = (owner[:, None] == owner[None, :]) & (index[None, :] < index[:, None])
    target = owner * capacity + jnp.sum(earlier.astype(jnp.int32), axis=1)
    slots = jnp.arange(members * capacity, dtype=jnp.int32)
    place = (slots[:, None] == target[None, :]).astype(BF16)
    return dot(place, old_rows).astype(BF16)


def covariance_of(old_rows, new_rows):
    features = old_rows.shape[1]
    half = features // 2
    core = lax.axis_index("core")
    mine = lax.dynamic_slice_in_dim(new_rows, core * half, half, 1)
    theirs = lax.dynamic_slice_in_dim(new_rows, (1 - core) * half, half, 1)
    old_pair = swap_core(old_rows)
    new_pair = swap_core(theirs)
    part = (dot(old_rows.T, mine) + dot(old_pair.T, new_pair)).astype(BF16)
    planes = lax.axis_size(SPREAD)
    block = features // planes
    arrived = exchange(part, SPREAD).reshape(planes, block, half)
    part = jnp.sum(arrived.astype(F32), axis=0).astype(BF16)
    depth = lax.axis_size("zh")
    copies = jnp.broadcast_to(part[None], (depth, block, half))
    arrived = exchange(copies, "zh").reshape(depth, block, half)
    total = jnp.sum(arrived.astype(F32), axis=0).astype(BF16)
    copies = jnp.broadcast_to(total[None], (planes // WIDTH, block, half))
    slab = exchange(copies.reshape(features // WIDTH, half), ("x", "zl"))
    return slab


def polar_kernel(place, *refs):
    owns, others = refs[0:WIDTH], refs[WIDTH : 2 * WIDTH]
    result, rotation = refs[2 * WIDTH : 2 * WIDTH + 2]
    start, middle, gram32, gram, poly = refs[2 * WIDTH + 2 :]
    rows, half = owns[0].shape
    features = 2 * half
    span = [slice(s * rows, (s + 1) * rows) for s in range(WIDTH)]
    pairs = [(s, t) for s in range(WIDTH) for t in range(s, WIDTH)]

    def product(a, b):
        return lax.dot_general(a, b, (((1,), (1,)), ((), ())), preferred_element_type=F32)

    def mirrored(target, s, t, value):
        target[span[s], span[t]] = value.astype(BF16)
        if s != t:
            target[span[t], span[s]] = value.T.astype(BF16)

    for s in range(WIDTH):
        start[span[s], :half] = owns[s][...]
        start[span[s], half:] = others[s][...]
    squares = jnp.zeros((1, 1), F32)
    diagonal = lax.broadcasted_iota(jnp.int32, (rows, rows), 0) == lax.broadcasted_iota(
        jnp.int32, (rows, rows), 1
    )
    for k, (s, t) in enumerate(pairs):
        value = product(start[span[s], :], start[span[t], :])
        gram32[k] = value
        if s == t:
            squares += jnp.sum(jnp.where(diagonal, value, 0.0), keepdims=True)
    scale = 0.25 * math.sqrt(features) / jnp.sqrt(squares + EPSILON)
    for k, (s, t) in enumerate(pairs):
        mirrored(gram, s, t, gram32[k] * (scale * scale))

    def polynomial():
        for s, t in pairs:
            square = product(gram[span[s], :], gram[span[t], :])
            mirrored(poly, s, t, COEFF_THREE * gram[span[s], span[t]].astype(F32) + COEFF_FIVE * square)

    def advance(source, s):
        moved = jnp.dot(poly[span[s], :], source[...], preferred_element_type=F32)
        return COEFF_ONE * source[span[s], :].astype(F32) + moved

    polynomial()
    for s in range(WIDTH):
        middle[span[s], :] = (advance(start, s) * scale).astype(BF16)
    for s, t in pairs:
        mirrored(gram, s, t, product(middle[span[s], :], middle[span[t], :]))
    polynomial()
    y, core, member = place[0], place[1], place[2]
    for s in range(WIDTH):
        first = pl.multiple_of(lax.rem(y - s + WIDTH, WIDTH) * rows, rows)
        value = advance(middle, s).astype(BF16)
        result[pl.ds(first, rows), pl.ds(pl.multiple_of(core * half, half), half)] = value[:, :half]
        result[pl.ds(first, rows), pl.ds(pl.multiple_of((1 - core) * half, half), half)] = value[:, half:]
    kept = rotation.shape[0]
    rotation[...] = result[pl.ds(pl.multiple_of(member * kept, kept), kept), :]


def polar(place, owns, others, block_rows):
    rows, half = owns[0].shape
    features = 2 * half
    whole = (features, features)

    vmem = pl.BlockSpec(memory_space=pltpu.VMEM)
    return pl.pallas_call(
        polar_kernel,
        out_shape=(
            jax.ShapeDtypeStruct(whole, BF16),
            jax.ShapeDtypeStruct((block_rows, features), BF16),
        ),
        in_specs=[pl.BlockSpec(memory_space=pltpu.SMEM)] + [vmem] * (2 * WIDTH),
        out_specs=(vmem, vmem),
        scratch_shapes=[
            pltpu.VMEM(whole, BF16),
            pltpu.VMEM(whole, BF16),
            pltpu.VMEM((WIDTH * (WIDTH + 1) // 2, rows, rows), F32),
            pltpu.VMEM(whole, BF16),
            pltpu.VMEM(whole, BF16),
        ],
        compiler_params=pltpu.CompilerParams(vmem_limit_bytes=24 * 1024 * 1024),
        cost_estimate=pl.CostEstimate(flops=9 * features**3, bytes_accessed=2**22, transcendentals=0),
        name="polar",
    )(place.astype(jnp.int32), *owns, *others)


def rotate_kernel(rows, factor, out):
    out[...] = jnp.dot(rows[...], factor[...], preferred_element_type=F32)


def rotate(rows, factor):
    count, features = rows.shape
    block = 128
    return pl.pallas_call(
        rotate_kernel,
        grid=(count // block,),
        out_shape=jax.ShapeDtypeStruct((count, features), F32),
        in_specs=[
            pl.BlockSpec((block, features), lambda i: (i, 0)),
            pl.BlockSpec((features, features), lambda i: (0, 0)),
        ],
        out_specs=pl.BlockSpec((block, features), lambda i: (i, 0)),
        compiler_params=pltpu.CompilerParams(vmem_limit_bytes=12 * 1024 * 1024),
        cost_estimate=pl.CostEstimate(
            flops=2 * count * features**2, bytes_accessed=5 * 2**20, transcendentals=0
        ),
        name="rotate",
    )(rows, factor)


def local(old_rows, new_rows, list_ids, owner_map):
    features = old_rows.shape[1]
    members = lax.axis_size(MEM)
    sent = outgoing_rows(old_rows, list_ids, owner_map, members)
    slab = covariance_of(old_rows, new_rows)
    slab, sent = lax.optimization_barrier((slab, sent))
    received = exchange(sent, MEM)
    owns = [slab]
    for shift in range(1, WIDTH):
        owns.append(lax.ppermute(slab, "y", [(i, (i + shift) % WIDTH) for i in range(WIDTH)]))
    others = [swap_core(own) for own in owns]
    place = jnp.stack([lax.axis_index("y"), lax.axis_index("core"), lax.axis_index(MEM)])
    factor, own_rows = polar(place, owns, others, features // members)
    return (rotate(received, factor), own_rows)


def solution(mesh):
    shape = mesh.shape
    grid = mesh.devices.reshape(WIDTH, 2, 4, shape["mem"] // 8, 2)
    fine = Mesh(grid, ALL)
    in_specs = (P(ALL, None), P(ALL, None), P(ALL), P())
    out_specs = (P(ALL, None), P(MEM, None))
    return jax.shard_map(local, mesh=fine, in_specs=in_specs, out_specs=out_specs, check_vma=False)
```

```python
import math

import jax
import jax.numpy as jnp
from jax import lax
from jax.experimental import pallas as pl
from jax.experimental.pallas import tpu as pltpu
from jax.sharding import Mesh
from jax.sharding import PartitionSpec as P

WIDTH = 4

EPSILON = 1e-06
COEFF_ONE = 3.4445
COEFF_THREE = -4.775
COEFF_FIVE = 2.0315

ALL = ("y", "core", "x", "zh", "zl")
MEM = ("x", "zh", "zl")
SPREAD = ("y", "x", "zl")
F32 = jnp.float32
BF16 = jnp.bfloat16


def dot(a, b):
    return jnp.dot(a, b, preferred_element_type=F32)


def swap_core(value):
    return lax.ppermute(value, "core", [(0, 1), (1, 0)])


def exchange(value, axes):
    return lax.all_to_all(value, axes, split_axis=0, concat_axis=0, tiled=True)


def outgoing_rows(old_rows, list_ids, owner_map, members):
    row_total = old_rows.shape[0]
    capacity = 2 * row_total // members
    owner = owner_map[list_ids]
    index = jnp.arange(row_total, dtype=jnp.int32)
    earlier = (owner[:, None] == owner[None, :]) & (index[None, :] < index[:, None])
    target = owner * capacity + jnp.sum(earlier.astype(jnp.int32), axis=1)
    slots = jnp.arange(members * capacity, dtype=jnp.int32)
    place = (slots[:, None] == target[None, :]).astype(BF16)
    return dot(place, old_rows).astype(BF16)


def product_kernel(place, old_own, new_own, old_pair, new_pair, out):
    features, half = out.shape
    block = features // 4
    mine = new_own[:, pl.ds(pl.multiple_of(place[1] * half, half), half)]
    for k in range(4):
        columns = slice(k * block, (k + 1) * block)
        total = None
        for old, new in ((old_own, mine), (old_pair, new_pair[...])):
            term = lax.dot_general(
                old[:, columns], new, (((0,), (0,)), ((), ())), preferred_element_type=F32
            )
            total = term if total is None else total + term
        out[columns, :] = total.astype(BF16)


def pair_product(place, old_own, new_own, old_pair, new_pair):
    rows, features = old_own.shape
    half = features // 2
    vmem = pl.BlockSpec(memory_space=pltpu.VMEM)
    return pl.pallas_call(
        product_kernel,
        out_shape=jax.ShapeDtypeStruct((features, half), BF16),
        in_specs=[pl.BlockSpec(memory_space=pltpu.SMEM)] + [vmem] * 4,
        out_specs=vmem,
        compiler_params=pltpu.CompilerParams(vmem_limit_bytes=12 * 1024 * 1024),
        cost_estimate=pl.CostEstimate(
            flops=4 * rows * features * half, bytes_accessed=3 * 2**20, transcendentals=0
        ),
        name="pair_product",
    )(place, old_own, new_own, old_pair, new_pair)


def sum_kernel(terms, out):
    total = terms[0].astype(F32)
    for k in range(1, terms.shape[0]):
        total += terms[k].astype(F32)
    for k in range(out.shape[0]):
        out[k] = total.astype(BF16)


def sum_and_copy(terms, copies):
    _, rows, columns = terms.shape
    vmem = pl.BlockSpec(memory_space=pltpu.VMEM)
    return pl.pallas_call(
        sum_kernel,
        out_shape=jax.ShapeDtypeStruct((copies, rows, columns), BF16),
        in_specs=[vmem],
        out_specs=vmem,
        compiler_params=pltpu.CompilerParams(vmem_limit_bytes=8 * 1024 * 1024),
        cost_estimate=pl.CostEstimate(flops=terms.size, bytes_accessed=2**20, transcendentals=0),
        name="sum_and_copy",
    )(terms)


def covariance_slab(place, old_rows, new_rows):
    features = old_rows.shape[1]
    half = features // 2
    core = lax.axis_index("core")
    theirs = lax.dynamic_slice_in_dim(new_rows, (1 - core) * half, half, 1)
    part = pair_product(place, old_rows, new_rows, swap_core(old_rows), swap_core(theirs))
    planes = lax.axis_size(SPREAD)
    depth = lax.axis_size("zh")
    block = features // planes
    arrived = exchange(part, SPREAD).reshape(planes, block, half)
    copies = sum_and_copy(arrived, depth)
    arrived = exchange(copies, "zh").reshape(depth, block, half)
    copies = sum_and_copy(arrived, planes // WIDTH)
    return exchange(copies.reshape(features // WIDTH, half), ("x", "zl"))


def polar_kernel(place, *refs):
    owns, others = refs[0:WIDTH], refs[WIDTH : 2 * WIDTH]
    result, rotation = refs[2 * WIDTH : 2 * WIDTH + 2]
    start, middle, gram32, gram, poly, slab_sem = refs[2 * WIDTH + 2 :]
    rows, half = owns[0].shape
    features = 2 * half
    span = [slice(s * rows, (s + 1) * rows) for s in range(WIDTH)]
    pairs = [(s, t) for s in range(WIDTH) for t in range(s, WIDTH)]

    def product(a, b):
        return lax.dot_general(a, b, (((1,), (1,)), ((), ())), preferred_element_type=F32)

    def mirrored(target, s, t, value):
        target[span[s], span[t]] = value.astype(BF16)
        if s != t:
            target[span[t], span[s]] = value.T.astype(BF16)

    own_slab = pltpu.make_async_copy(owns[0], start.at[span[0], pl.ds(0, half)], slab_sem)
    own_slab.start()
    for s in range(WIDTH):
        if s:
            start[span[s], :half] = owns[s][...]
        start[span[s], half:] = others[s][...]
    own_slab.wait()
    squares = jnp.zeros((1, 1), F32)
    diagonal = lax.broadcasted_iota(jnp.int32, (rows, rows), 0) == lax.broadcasted_iota(
        jnp.int32, (rows, rows), 1
    )
    for k, (s, t) in enumerate(pairs):
        value = product(start[span[s], :], start[span[t], :])
        gram32[k] = value
        if s == t:
            squares += jnp.sum(jnp.where(diagonal, value, 0.0), keepdims=True)
    scale = 0.25 * math.sqrt(features) / jnp.sqrt(squares + EPSILON)
    for k, (s, t) in enumerate(pairs):
        mirrored(gram, s, t, gram32[k] * (scale * scale))

    def polynomial():
        for s, t in pairs:
            square = product(gram[span[s], :], gram[span[t], :])
            mirrored(poly, s, t, COEFF_THREE * gram[span[s], span[t]].astype(F32) + COEFF_FIVE * square)

    def advance(source, s):
        moved = jnp.dot(poly[span[s], :], source[...], preferred_element_type=F32)
        return COEFF_ONE * source[span[s], :].astype(F32) + moved

    polynomial()
    for s in range(WIDTH):
        middle[span[s], :] = (advance(start, s) * scale).astype(BF16)
    for s, t in pairs:
        mirrored(gram, s, t, product(middle[span[s], :], middle[span[t], :]))
    polynomial()
    y, core, member = place[0], place[1], place[2]
    for s in range(WIDTH):
        first = pl.multiple_of(lax.rem(y - s + WIDTH, WIDTH) * rows, rows)
        value = advance(middle, s).astype(BF16)
        result[pl.ds(first, rows), pl.ds(pl.multiple_of(core * half, half), half)] = value[:, :half]
        result[pl.ds(first, rows), pl.ds(pl.multiple_of((1 - core) * half, half), half)] = value[:, half:]
    kept = rotation.shape[0]
    rotation[...] = result[pl.ds(pl.multiple_of(member * kept, kept), kept), :]


def polar(place, owns, others, block_rows):
    rows, half = owns[0].shape
    features = 2 * half
    whole = (features, features)

    vmem = pl.BlockSpec(memory_space=pltpu.VMEM)
    return pl.pallas_call(
        polar_kernel,
        out_shape=(
            jax.ShapeDtypeStruct(whole, BF16),
            jax.ShapeDtypeStruct((block_rows, features), BF16),
        ),
        in_specs=[pl.BlockSpec(memory_space=pltpu.SMEM), pl.BlockSpec(memory_space=pl.ANY)]
        + [vmem] * (2 * WIDTH - 1),
        out_specs=(vmem, vmem),
        scratch_shapes=[
            pltpu.VMEM(whole, BF16),
            pltpu.VMEM(whole, BF16),
            pltpu.VMEM((WIDTH * (WIDTH + 1) // 2, rows, rows), F32),
            pltpu.VMEM(whole, BF16),
            pltpu.VMEM(whole, BF16),
            pltpu.SemaphoreType.DMA,
        ],
        compiler_params=pltpu.CompilerParams(vmem_limit_bytes=24 * 1024 * 1024),
        cost_estimate=pl.CostEstimate(flops=9 * features**3, bytes_accessed=2**22, transcendentals=0),
        name="polar",
    )(place, *owns, *others)


def rotate_kernel(rows, factor, out, held, product, in_sems, out_sems):
    block = held.shape[1]
    parts = range(held.shape[0])

    def fetch(k):
        return pltpu.make_async_copy(rows.at[pl.ds(k * block, block), :], held.at[k], in_sems.at[k])

    def store(k):
        return pltpu.make_async_copy(product.at[k], out.at[pl.ds(k * block, block), :], out_sems.at[k])

    for k in parts:
        fetch(k).start()
    for k in parts:
        fetch(k).wait()
        product[k] = jnp.dot(held[k], factor[...], preferred_element_type=F32)
        store(k).start()
    for k in parts:
        store(k).wait()


def rotate(rows, factor):
    count, features = rows.shape
    parts = 4
    block = count // parts
    return pl.pallas_call(
        rotate_kernel,
        out_shape=jax.ShapeDtypeStruct((count, features), F32),
        in_specs=[pl.BlockSpec(memory_space=pltpu.HBM), pl.BlockSpec(memory_space=pltpu.VMEM)],
        out_specs=pl.BlockSpec(memory_space=pltpu.HBM),
        scratch_shapes=[
            pltpu.VMEM((parts, block, features), BF16),
            pltpu.VMEM((parts, block, features), F32),
            pltpu.SemaphoreType.DMA((parts,)),
            pltpu.SemaphoreType.DMA((parts,)),
        ],
        compiler_params=pltpu.CompilerParams(vmem_limit_bytes=12 * 1024 * 1024),
        cost_estimate=pl.CostEstimate(
            flops=2 * count * features**2, bytes_accessed=5 * 2**20, transcendentals=0
        ),
        name="rotate",
    )(rows, factor)


def local(old_rows, new_rows, list_ids, owner_map):
    features = old_rows.shape[1]
    members = lax.axis_size(MEM)
    place = jnp.stack([lax.axis_index("y"), lax.axis_index("core"), lax.axis_index(MEM)])
    place = place.astype(jnp.int32)
    sent = outgoing_rows(old_rows, list_ids, owner_map, members)
    slab = covariance_slab(place, old_rows, new_rows)
    slab, sent = lax.optimization_barrier((slab, sent))
    received = exchange(sent, MEM)
    owns = [slab]
    for shift in range(1, WIDTH):
        owns.append(lax.ppermute(slab, "y", [(i, (i + shift) % WIDTH) for i in range(WIDTH)]))
    others = [swap_core(own) for own in owns]
    factor, own_rows = polar(place, owns, others, features // members)
    return (rotate(received, factor), own_rows)


def solution(mesh):
    shape = mesh.shape
    grid = mesh.devices.reshape(WIDTH, 2, 4, shape["mem"] // 8, 2)
    fine = Mesh(grid, ALL)
    in_specs = (P(ALL, None), P(ALL, None), P(ALL), P())
    out_specs = (P(ALL, None), P(MEM, None))
    return jax.shard_map(local, mesh=fine, in_specs=in_specs, out_specs=out_specs, check_vma=False)
```

```python
import math

import jax
import jax.numpy as jnp
from jax import lax
from jax.experimental import pallas as pl
from jax.experimental.pallas import tpu as pltpu
from jax.sharding import Mesh
from jax.sharding import PartitionSpec as P

WIDTH = 4

EPSILON = 1e-06
COEFF_ONE = 3.4445
COEFF_THREE = -4.775
COEFF_FIVE = 2.0315

Y = ("yh", "yl")
ALL = ("yh", "yl", "core", "x", "zh", "zl")
MEM = ("x", "zh", "zl")
SPREAD = ("yh", "yl", "x", "zl")
GATHER = ("yh", "x", "zl")
F32 = jnp.float32
BF16 = jnp.bfloat16


def dot(a, b):
    return jnp.dot(a, b, preferred_element_type=F32)


def swap_core(value):
    return lax.ppermute(value, "core", [(0, 1), (1, 0)])


def exchange(value, axes):
    return lax.all_to_all(value, axes, split_axis=0, concat_axis=0, tiled=True)


def outgoing_rows(old_rows, list_ids, owner_map, members):
    row_total = old_rows.shape[0]
    capacity = 2 * row_total // members
    owner = owner_map[list_ids]
    index = jnp.arange(row_total, dtype=jnp.int32)
    earlier = (owner[:, None] == owner[None, :]) & (index[None, :] < index[:, None])
    target = owner * capacity + jnp.sum(earlier.astype(jnp.int32), axis=1)
    slots = jnp.arange(members * capacity, dtype=jnp.int32)
    place = (slots[:, None] == target[None, :]).astype(BF16)
    return dot(place, old_rows).astype(BF16)


def sum_kernel(terms, out):
    total = terms[0].astype(F32)
    for k in range(1, terms.shape[0]):
        total += terms[k].astype(F32)
    for k in range(out.shape[0]):
        out[k] = total.astype(BF16)


def sum_and_copy(terms, copies):
    _, rows, columns = terms.shape
    vmem = pl.BlockSpec(memory_space=pltpu.VMEM)
    return pl.pallas_call(
        sum_kernel,
        out_shape=jax.ShapeDtypeStruct((copies, rows, columns), BF16),
        in_specs=[vmem],
        out_specs=vmem,
        compiler_params=pltpu.CompilerParams(vmem_limit_bytes=8 * 1024 * 1024),
        cost_estimate=pl.CostEstimate(flops=terms.size, bytes_accessed=2**20, transcendentals=0),
        name="sum_and_copy",
    )(terms)


def covariance_slabs(old_rows, new_rows):
    features = old_rows.shape[1]
    half = features // 2
    core = lax.axis_index("core")
    mine = lax.dynamic_slice_in_dim(new_rows, core * half, half, 1)
    theirs = lax.dynamic_slice_in_dim(new_rows, (1 - core) * half, half, 1)
    old_pair = swap_core(old_rows)
    new_pair = swap_core(theirs)
    part = (dot(old_rows.T, mine) + dot(old_pair.T, new_pair)).astype(BF16)
    planes = lax.axis_size(SPREAD)
    depth = lax.axis_size("zh")
    gathered = lax.axis_size(GATHER)
    block = features // planes
    arrived = exchange(part, SPREAD).reshape(planes, block, half)
    copies = sum_and_copy(arrived, depth)
    arrived = exchange(copies, "zh").reshape(depth, block, half)
    copies = sum_and_copy(arrived, gathered)
    return exchange(copies.reshape(gathered * block, half), GATHER)


def polar_kernel(place, mine, got_low, got_high, mine_other, low_other, high_other, *refs):
    result, rotation, start, middle, gram32, gram, poly, sems, out_sems = refs
    rows, half = got_low.shape
    features = 2 * half
    span = [slice(s * rows, (s + 1) * rows) for s in range(WIDTH)]
    pairs = [(s, t) for s in range(WIDTH) for t in range(s, WIDTH)]

    def product(a, b):
        return lax.dot_general(a, b, (((1,), (1,)), ((), ())), preferred_element_type=F32)

    def mirrored(target, s, t, value):
        target[span[s], span[t]] = value.astype(BF16)
        if s != t:
            target[span[t], span[s]] = value.T.astype(BF16)

    arrivals = [
        pltpu.make_async_copy(
            part, start.at[pl.ds(first * rows, part.shape[0]), pl.ds(side * half, half)], sems.at[k]
        )
        for k, (part, first, side) in enumerate(
            (
                (mine, 0, 0),
                (mine_other, 0, 1),
                (got_low, 2, 0),
                (low_other, 2, 1),
                (got_high, 3, 0),
                (high_other, 3, 1),
            )
        )
    ]
    for arrival in arrivals:
        arrival.start()
    for arrival in arrivals:
        arrival.wait()
    squares = jnp.zeros((1, 1), F32)
    diagonal = lax.broadcasted_iota(jnp.int32, (rows, rows), 0) == lax.broadcasted_iota(
        jnp.int32, (rows, rows), 1
    )
    for k, (s, t) in enumerate(pairs):
        value = product(start[span[s], :], start[span[t], :])
        gram32[k] = value
        if s == t:
            squares += jnp.sum(jnp.where(diagonal, value, 0.0), keepdims=True)
    scale = 0.25 * math.sqrt(features) / jnp.sqrt(squares + EPSILON)
    for k, (s, t) in enumerate(pairs):
        mirrored(gram, s, t, gram32[k] * (scale * scale))

    def polynomial():
        for s, t in pairs:
            square = product(gram[span[s], :], gram[span[t], :])
            mirrored(poly, s, t, COEFF_THREE * gram[span[s], span[t]].astype(F32) + COEFF_FIVE * square)

    def advance(source, s):
        moved = jnp.dot(poly[span[s], :], source[...], preferred_element_type=F32)
        return COEFF_ONE * source[span[s], :].astype(F32) + moved

    polynomial()
    for s in range(WIDTH):
        middle[span[s], :] = (advance(start, s) * scale).astype(BF16)
    for s, t in pairs:
        mirrored(gram, s, t, product(middle[span[s], :], middle[span[t], :]))
    polynomial()
    low, core, member = place[0], place[1], place[2]
    order = (low, low + 2, 1 - low, 3 - low)
    stores = []
    for s in range(WIDTH):
        first = pl.multiple_of(order[s] * rows, rows)
        value = advance(middle, s).astype(BF16)
        start[pl.ds(first, rows), pl.ds(pl.multiple_of(core * half, half), half)] = value[:, :half]
        start[pl.ds(first, rows), pl.ds(pl.multiple_of((1 - core) * half, half), half)] = value[:, half:]
        slab = pl.ds(first, rows)
        stores.append(pltpu.make_async_copy(start.at[slab, :], result.at[slab, :], out_sems.at[s]))
        stores[s].start()
    kept = rotation.shape[0]
    rotation[...] = start[pl.ds(pl.multiple_of(member * kept, kept), kept), :]
    for store in stores:
        store.wait()


def polar(place, parts, block_rows):
    rows, half = parts[1].shape
    features = 2 * half
    whole = (features, features)
    vmem = pl.BlockSpec(memory_space=pltpu.VMEM)
    return pl.pallas_call(
        polar_kernel,
        out_shape=(
            pltpu.HBM(whole, BF16),
            jax.ShapeDtypeStruct((block_rows, features), BF16),
        ),
        in_specs=[pl.BlockSpec(memory_space=pltpu.SMEM)]
        + [pl.BlockSpec(memory_space=pl.ANY)] * len(parts),
        out_specs=(pl.BlockSpec(memory_space=pl.ANY), vmem),
        scratch_shapes=[
            pltpu.VMEM(whole, BF16),
            pltpu.VMEM(whole, BF16),
            pltpu.VMEM((WIDTH * (WIDTH + 1) // 2, rows, rows), F32),
            pltpu.VMEM(whole, BF16),
            pltpu.VMEM(whole, BF16),
            pltpu.SemaphoreType.DMA((len(parts),)),
            pltpu.SemaphoreType.DMA((WIDTH,)),
        ],
        compiler_params=pltpu.CompilerParams(vmem_limit_bytes=24 * 1024 * 1024),
        cost_estimate=pl.CostEstimate(flops=9 * features**3, bytes_accessed=2**22, transcendentals=0),
        name="polar",
    )(place, *parts)


def rotate_kernel(rows, factor, out, held, weights, product, row_sem, in_sems, out_sems):
    block = held.shape[1] // in_sems.shape[0]
    parts = range(in_sems.shape[0])
    columns = [pl.ds(k * block, block) for k in parts]

    def fetch(k):
        return pltpu.make_async_copy(factor.at[:, columns[k]], weights.at[:, columns[k]], in_sems.at[k])

    def store(k):
        return pltpu.make_async_copy(product.at[:, columns[k]], out.at[:, columns[k]], out_sems.at[k])

    row_copy = pltpu.make_async_copy(rows, held, row_sem)
    fetch(0).start()
    row_copy.start()
    for k in parts[1:]:
        fetch(k).start()
    row_copy.wait()
    for k in parts:
        fetch(k).wait()
        product[:, columns[k]] = jnp.dot(held[...], weights[:, columns[k]], preferred_element_type=F32)
        store(k).start()
    for k in parts:
        store(k).wait()


def rotate(rows, factor):
    count, features = rows.shape
    parts = 4
    anywhere = pl.BlockSpec(memory_space=pl.ANY)
    return pl.pallas_call(
        rotate_kernel,
        out_shape=jax.ShapeDtypeStruct((count, features), F32),
        in_specs=[anywhere, anywhere],
        out_specs=anywhere,
        scratch_shapes=[
            pltpu.VMEM((count, features), BF16),
            pltpu.VMEM((features, features), BF16),
            pltpu.VMEM((count, features), F32),
            pltpu.SemaphoreType.DMA,
            pltpu.SemaphoreType.DMA((parts,)),
            pltpu.SemaphoreType.DMA((parts,)),
        ],
        compiler_params=pltpu.CompilerParams(vmem_limit_bytes=12 * 1024 * 1024),
        cost_estimate=pl.CostEstimate(
            flops=2 * count * features**2, bytes_accessed=5 * 2**20, transcendentals=0
        ),
        name="rotate",
    )(rows, factor)


def local(old_rows, new_rows, list_ids, owner_map):
    features = old_rows.shape[1]
    members = lax.axis_size(MEM)
    place = jnp.stack([lax.axis_index("yl"), lax.axis_index("core"), lax.axis_index(MEM)])
    sent = outgoing_rows(old_rows, list_ids, owner_map, members)
    mine = covariance_slabs(old_rows, new_rows)
    mine, sent = lax.optimization_barrier((mine, sent))
    received = exchange(sent, MEM)
    rows = mine.shape[0] // 2
    up = [(i, (i + 1) % WIDTH) for i in range(WIDTH)]
    down = [(i, (i - 1) % WIDTH) for i in range(WIDTH)]
    parts = [mine, lax.ppermute(mine[:rows], Y, up), lax.ppermute(mine[rows:], Y, down)]
    parts += [swap_core(part) for part in parts]
    factor, own_rows = polar(place.astype(jnp.int32), parts, features // members)
    factor = pltpu.with_memory_space_constraint(factor, pltpu.HBM)
    return (rotate(received, factor), own_rows)


def solution(mesh):
    shape = mesh.shape
    grid = mesh.devices.reshape(2, WIDTH // 2, 2, 4, shape["mem"] // 8, 2)
    fine = Mesh(grid, ALL)
    in_specs = (P(ALL, None), P(ALL, None), P(ALL), P())
    out_specs = (P(ALL, None), P(MEM, None))
    return jax.shard_map(local, mesh=fine, in_specs=in_specs, out_specs=out_specs, check_vma=False)
```

```python
import math

import jax
import jax.numpy as jnp
from jax import lax
from jax.experimental import pallas as pl
from jax.experimental.pallas import tpu as pltpu
from jax.sharding import Mesh
from jax.sharding import PartitionSpec as P

WIDTH = 4

EPSILON = 1e-06
COEFF_ONE = 3.4445
COEFF_THREE = -4.775
COEFF_FIVE = 2.0315

Y = ("yh", "yl")
ALL = ("yh", "yl", "core", "x", "zh", "zl")
MEM = ("x", "zh", "zl")
SPREAD = ("yh", "yl", "x", "zl")
GATHER = ("yh", "x", "zl")
F32 = jnp.float32
BF16 = jnp.bfloat16


def dot(a, b):
    return jnp.dot(a, b, preferred_element_type=F32)


def swap_core(value):
    return lax.ppermute(value, "core", [(0, 1), (1, 0)])


def exchange(value, axes):
    return lax.all_to_all(value, axes, split_axis=0, concat_axis=0, tiled=True)


def outgoing_rows(old_rows, list_ids, owner_map, members):
    row_total = old_rows.shape[0]
    capacity = 2 * row_total // members
    owner = owner_map[list_ids]
    index = jnp.arange(row_total, dtype=jnp.int32)
    earlier = (owner[:, None] == owner[None, :]) & (index[None, :] < index[:, None])
    target = owner * capacity + jnp.sum(earlier.astype(jnp.int32), axis=1)
    slots = jnp.arange(members * capacity, dtype=jnp.int32)
    place = (slots[:, None] == target[None, :]).astype(BF16)
    return dot(place, old_rows).astype(BF16)


def sum_kernel(terms, out):
    total = terms[0].astype(F32)
    for k in range(1, terms.shape[0]):
        total += terms[k].astype(F32)
    for k in range(out.shape[0]):
        out[k] = total.astype(BF16)


def sum_and_copy(terms, copies):
    _, rows, columns = terms.shape
    vmem = pl.BlockSpec(memory_space=pltpu.VMEM)
    return pl.pallas_call(
        sum_kernel,
        out_shape=jax.ShapeDtypeStruct((copies, rows, columns), BF16),
        in_specs=[vmem],
        out_specs=vmem,
        compiler_params=pltpu.CompilerParams(vmem_limit_bytes=8 * 1024 * 1024),
        cost_estimate=pl.CostEstimate(flops=terms.size, bytes_accessed=2**20, transcendentals=0),
        name="sum_and_copy",
    )(terms)


def covariance_slabs(old_rows, new_rows):
    features = old_rows.shape[1]
    half = features // 2
    core = lax.axis_index("core")
    mine = lax.dynamic_slice_in_dim(new_rows, core * half, half, 1)
    theirs = lax.dynamic_slice_in_dim(new_rows, (1 - core) * half, half, 1)
    old_pair = swap_core(old_rows)
    new_pair = swap_core(theirs)
    part = (dot(old_rows.T, mine) + dot(old_pair.T, new_pair)).astype(BF16)
    planes = lax.axis_size(SPREAD)
    depth = lax.axis_size("zh")
    gathered = lax.axis_size(GATHER)
    block = features // planes
    arrived = exchange(part, SPREAD).reshape(planes, block, half)
    copies = sum_and_copy(arrived, depth)
    arrived = exchange(copies, "zh").reshape(depth, block, half)
    copies = sum_and_copy(arrived, gathered)
    return exchange(copies.reshape(gathered * block, half), GATHER)


def polar_kernel(place, mine, got_low, got_high, mine_other, low_other, high_other, *refs):
    result, rotation, start, middle, gram32, gram, poly, sems = refs
    rows, half = got_low.shape
    features = 2 * half
    span = [slice(s * rows, (s + 1) * rows) for s in range(WIDTH)]
    pairs = [(s, t) for t in range(WIDTH) for s in range(t + 1)]

    def product(a, b):
        return lax.dot_general(a, b, (((1,), (1,)), ((), ())), preferred_element_type=F32)

    def mirrored(target, s, t, value):
        target[span[s], span[t]] = value.astype(BF16)
        if s != t:
            target[span[t], span[s]] = value.T.astype(BF16)

    arrivals = [
        pltpu.make_async_copy(
            part, start.at[pl.ds(first * rows, part.shape[0]), pl.ds(side * half, half)], sems.at[k]
        )
        for k, (part, first, side) in enumerate(
            (
                (mine, 0, 0),
                (mine_other, 0, 1),
                (got_low, 2, 0),
                (low_other, 2, 1),
                (got_high, 3, 0),
                (high_other, 3, 1),
            )
        )
    ]
    for arrival in arrivals:
        arrival.start()
    squares = jnp.zeros((1, 1), F32)
    diagonal = lax.broadcasted_iota(jnp.int32, (rows, rows), 0) == lax.broadcasted_iota(
        jnp.int32, (rows, rows), 1
    )
    for k, (s, t) in enumerate(pairs):
        if s == 0 and t != 1:
            for arrival in arrivals[2 * max(t - 1, 0) : 2 * max(t - 1, 0) + 2]:
                arrival.wait()
        value = product(start[span[s], :], start[span[t], :])
        gram32[k] = value
        if s == t:
            squares += jnp.sum(jnp.where(diagonal, value, 0.0), keepdims=True)
    scale = 0.25 * math.sqrt(features) / jnp.sqrt(squares + EPSILON)
    for k, (s, t) in enumerate(pairs):
        mirrored(gram, s, t, gram32[k] * (scale * scale))

    def polynomial():
        for s, t in pairs:
            square = product(gram[span[s], :], gram[span[t], :])
            mirrored(poly, s, t, COEFF_THREE * gram[span[s], span[t]].astype(F32) + COEFF_FIVE * square)

    def advance(source, s):
        moved = jnp.dot(poly[span[s], :], source[...], preferred_element_type=F32)
        return COEFF_ONE * source[span[s], :].astype(F32) + moved

    polynomial()
    for s in range(WIDTH):
        middle[span[s], :] = (advance(start, s) * scale).astype(BF16)
    for s, t in pairs:
        mirrored(gram, s, t, product(middle[span[s], :], middle[span[t], :]))
    polynomial()
    low, core, member = place[0], place[1], place[2]
    order = (low, low + 2, 1 - low, 3 - low)
    for s in range(WIDTH):
        first = pl.multiple_of(order[s] * rows, rows)
        value = advance(middle, s).astype(BF16)
        result[pl.ds(first, rows), pl.ds(pl.multiple_of(core * half, half), half)] = value[:, :half]
        result[pl.ds(first, rows), pl.ds(pl.multiple_of((1 - core) * half, half), half)] = value[:, half:]
    kept = rotation.shape[0]
    rotation[...] = result[pl.ds(pl.multiple_of(member * kept, kept), kept), :]


def polar(place, parts, block_rows):
    rows, half = parts[1].shape
    features = 2 * half
    whole = (features, features)
    vmem = pl.BlockSpec(memory_space=pltpu.VMEM)
    return pl.pallas_call(
        polar_kernel,
        out_shape=(
            jax.ShapeDtypeStruct(whole, BF16),
            jax.ShapeDtypeStruct((block_rows, features), BF16),
        ),
        in_specs=[pl.BlockSpec(memory_space=pltpu.SMEM)]
        + [pl.BlockSpec(memory_space=pl.ANY)] * len(parts),
        out_specs=(vmem, vmem),
        scratch_shapes=[
            pltpu.VMEM(whole, BF16),
            pltpu.VMEM(whole, BF16),
            pltpu.VMEM((WIDTH * (WIDTH + 1) // 2, rows, rows), F32),
            pltpu.VMEM(whole, BF16),
            pltpu.VMEM(whole, BF16),
            pltpu.SemaphoreType.DMA((len(parts),)),
        ],
        compiler_params=pltpu.CompilerParams(vmem_limit_bytes=24 * 1024 * 1024),
        cost_estimate=pl.CostEstimate(flops=9 * features**3, bytes_accessed=2**22, transcendentals=0),
        name="polar",
    )(place, *parts)


def rotate_kernel(rows, factor, out, held, product, in_sems, out_sems):
    block = held.shape[1]
    parts = range(held.shape[0])

    def fetch(k):
        return pltpu.make_async_copy(rows.at[pl.ds(k * block, block), :], held.at[k], in_sems.at[k])

    def store(k):
        return pltpu.make_async_copy(product.at[k], out.at[pl.ds(k * block, block), :], out_sems.at[k])

    for k in parts:
        fetch(k).start()
    for k in parts:
        fetch(k).wait()
        product[k] = jnp.dot(held[k], factor[...], preferred_element_type=F32)
        store(k).start()
    for k in parts:
        store(k).wait()


def rotate(rows, factor):
    count, features = rows.shape
    parts = 4
    block = count // parts
    return pl.pallas_call(
        rotate_kernel,
        out_shape=jax.ShapeDtypeStruct((count, features), F32),
        in_specs=[pl.BlockSpec(memory_space=pltpu.HBM), pl.BlockSpec(memory_space=pltpu.VMEM)],
        out_specs=pl.BlockSpec(memory_space=pltpu.HBM),
        scratch_shapes=[
            pltpu.VMEM((parts, block, features), BF16),
            pltpu.VMEM((parts, block, features), F32),
            pltpu.SemaphoreType.DMA((parts,)),
            pltpu.SemaphoreType.DMA((parts,)),
        ],
        compiler_params=pltpu.CompilerParams(vmem_limit_bytes=12 * 1024 * 1024),
        cost_estimate=pl.CostEstimate(
            flops=2 * count * features**2, bytes_accessed=5 * 2**20, transcendentals=0
        ),
        name="rotate",
    )(rows, factor)


def local(old_rows, new_rows, list_ids, owner_map):
    features = old_rows.shape[1]
    members = lax.axis_size(MEM)
    place = jnp.stack([lax.axis_index("yl"), lax.axis_index("core"), lax.axis_index(MEM)])
    sent = outgoing_rows(old_rows, list_ids, owner_map, members)
    mine = covariance_slabs(old_rows, new_rows)
    mine, sent = lax.optimization_barrier((mine, sent))
    received = exchange(sent, MEM)
    rows = mine.shape[0] // 2
    up = [(i, (i + 1) % WIDTH) for i in range(WIDTH)]
    down = [(i, (i - 1) % WIDTH) for i in range(WIDTH)]
    parts = [mine, lax.ppermute(mine[:rows], Y, up), lax.ppermute(mine[rows:], Y, down)]
    parts += [swap_core(part) for part in parts]
    parts = [pltpu.with_memory_space_constraint(part, pltpu.HBM) for part in parts]
    factor, own_rows = polar(place.astype(jnp.int32), parts, features // members)
    received = pltpu.with_memory_space_constraint(received, pltpu.HBM)
    return (rotate(received, factor), own_rows)


def solution(mesh):
    shape = mesh.shape
    grid = mesh.devices.reshape(2, WIDTH // 2, 2, 4, shape["mem"] // 8, 2)
    fine = Mesh(grid, ALL)
    in_specs = (P(ALL, None), P(ALL, None), P(ALL), P())
    out_specs = (P(ALL, None), P(MEM, None))
    return jax.shard_map(local, mesh=fine, in_specs=in_specs, out_specs=out_specs, check_vma=False)
```

```python
import math

import jax
import jax.numpy as jnp
from jax import lax
from jax.experimental import pallas as pl
from jax.experimental.pallas import tpu as pltpu
from jax.sharding import Mesh
from jax.sharding import PartitionSpec as P

WIDTH = 4

EPSILON = 1e-06
COEFF_ONE = 3.4445
COEFF_THREE = -4.775
COEFF_FIVE = 2.0315

Y = ("yh", "yl")
ALL = ("yh", "yl", "core", "x", "zh", "zl")
MEM = ("x", "zh", "zl")
SPREAD = ("yh", "yl", "x", "zl")
GATHER = ("yh", "x", "zl")
F32 = jnp.float32
BF16 = jnp.bfloat16


def dot(a, b):
    return jnp.dot(a, b, preferred_element_type=F32)


def swap_core(value):
    return lax.ppermute(value, "core", [(0, 1), (1, 0)])


def exchange(value, axes):
    return lax.all_to_all(value, axes, split_axis=0, concat_axis=0, tiled=True)


def outgoing_rows(old_rows, list_ids, owner_map, members):
    row_total = old_rows.shape[0]
    capacity = 2 * row_total // members
    owner = owner_map[list_ids]
    index = jnp.arange(row_total, dtype=jnp.int32)
    earlier = (owner[:, None] == owner[None, :]) & (index[None, :] < index[:, None])
    target = owner * capacity + jnp.sum(earlier.astype(jnp.int32), axis=1)
    slots = jnp.arange(members * capacity, dtype=jnp.int32)
    place = (slots[:, None] == target[None, :]).astype(BF16)
    return dot(place, old_rows).astype(BF16)


def sum_kernel(terms, out):
    total = terms[0].astype(F32)
    for k in range(1, terms.shape[0]):
        total += terms[k].astype(F32)
    for k in range(out.shape[0]):
        out[k] = total.astype(BF16)


def sum_and_copy(terms, copies):
    _, rows, columns = terms.shape
    vmem = pl.BlockSpec(memory_space=pltpu.VMEM)
    return pl.pallas_call(
        sum_kernel,
        out_shape=jax.ShapeDtypeStruct((copies, rows, columns), BF16),
        in_specs=[vmem],
        out_specs=vmem,
        compiler_params=pltpu.CompilerParams(vmem_limit_bytes=8 * 1024 * 1024),
        cost_estimate=pl.CostEstimate(flops=terms.size, bytes_accessed=2**20, transcendentals=0),
        name="sum_and_copy",
    )(terms)


def covariance_slabs(old_rows, new_rows):
    features = old_rows.shape[1]
    half = features // 2
    core = lax.axis_index("core")
    mine = lax.dynamic_slice_in_dim(new_rows, core * half, half, 1)
    theirs = lax.dynamic_slice_in_dim(new_rows, (1 - core) * half, half, 1)
    old_pair = swap_core(old_rows)
    new_pair = swap_core(theirs)
    part = (dot(old_rows.T, mine) + dot(old_pair.T, new_pair)).astype(BF16)
    planes = lax.axis_size(SPREAD)
    depth = lax.axis_size("zh")
    gathered = lax.axis_size(GATHER)
    block = features // planes
    arrived = exchange(part, SPREAD).reshape(planes, block, half)
    copies = sum_and_copy(arrived, depth)
    arrived = exchange(copies, "zh").reshape(depth, block, half)
    copies = sum_and_copy(arrived, gathered)
    return exchange(copies.reshape(gathered * block, half), GATHER)


def polar_kernel(place, mine, got_low, got_high, mine_other, low_other, high_other, *refs):
    result, rotation, start, middle, gram32, gram, poly, sems = refs
    rows, half = got_low.shape
    features = 2 * half
    span = [slice(s * rows, (s + 1) * rows) for s in range(WIDTH)]
    pairs = [(s, t) for t in range(WIDTH) for s in range(t + 1)]

    def product(a, b):
        return lax.dot_general(a, b, (((1,), (1,)), ((), ())), preferred_element_type=F32)

    def mirrored(target, s, t, value):
        target[span[s], span[t]] = value.astype(BF16)
        if s != t:
            target[span[t], span[s]] = value.T.astype(BF16)

    arrivals = [
        pltpu.make_async_copy(
            part, start.at[pl.ds(first * rows, part.shape[0]), pl.ds(side * half, half)], sems.at[k]
        )
        for k, (part, first, side) in enumerate(
            (
                (mine, 0, 0),
                (mine_other, 0, 1),
                (got_low, 2, 0),
                (low_other, 2, 1),
                (got_high, 3, 0),
                (high_other, 3, 1),
            )
        )
    ]
    for arrival in arrivals:
        arrival.start()
    squares = jnp.zeros((1, 1), F32)
    diagonal = lax.broadcasted_iota(jnp.int32, (rows, rows), 0) == lax.broadcasted_iota(
        jnp.int32, (rows, rows), 1
    )
    for k, (s, t) in enumerate(pairs):
        if s == 0 and t != 1:
            for arrival in arrivals[2 * max(t - 1, 0) : 2 * max(t - 1, 0) + 2]:
                arrival.wait()
        value = product(start[span[s], :], start[span[t], :])
        gram32[k] = value
        if s == t:
            squares += jnp.sum(jnp.where(diagonal, value, 0.0), keepdims=True)
    scale = 0.25 * math.sqrt(features) / jnp.sqrt(squares + EPSILON)
    for k, (s, t) in enumerate(pairs):
        mirrored(gram, s, t, gram32[k] * (scale * scale))

    def polynomial():
        for s, t in pairs:
            square = product(gram[span[s], :], gram[span[t], :])
            mirrored(poly, s, t, COEFF_THREE * gram[span[s], span[t]].astype(F32) + COEFF_FIVE * square)

    def advance(source, s):
        moved = jnp.dot(poly[span[s], :], source[...], preferred_element_type=F32)
        return COEFF_ONE * source[span[s], :].astype(F32) + moved

    polynomial()
    for s in range(WIDTH):
        middle[span[s], :] = (advance(start, s) * scale).astype(BF16)
    for s, t in pairs:
        mirrored(gram, s, t, product(middle[span[s], :], middle[span[t], :]))
    polynomial()
    low, core, member = place[0], place[1], place[2]
    order = (low, low + 2, 1 - low, 3 - low)
    for s in range(WIDTH):
        first = pl.multiple_of(order[s] * rows, rows)
        value = advance(middle, s).astype(BF16)
        result[pl.ds(first, rows), pl.ds(pl.multiple_of(core * half, half), half)] = value[:, :half]
        result[pl.ds(first, rows), pl.ds(pl.multiple_of((1 - core) * half, half), half)] = value[:, half:]
    kept = rotation.shape[0]
    rotation[...] = result[pl.ds(pl.multiple_of(member * kept, kept), kept), :]


def polar(place, parts, block_rows):
    rows, half = parts[1].shape
    features = 2 * half
    whole = (features, features)
    vmem = pl.BlockSpec(memory_space=pltpu.VMEM)
    return pl.pallas_call(
        polar_kernel,
        out_shape=(
            jax.ShapeDtypeStruct(whole, BF16),
            jax.ShapeDtypeStruct((block_rows, features), BF16),
        ),
        in_specs=[pl.BlockSpec(memory_space=pltpu.SMEM)]
        + [pl.BlockSpec(memory_space=pl.ANY)] * len(parts),
        out_specs=(vmem, vmem),
        scratch_shapes=[
            pltpu.VMEM(whole, BF16),
            pltpu.VMEM(whole, BF16),
            pltpu.VMEM((WIDTH * (WIDTH + 1) // 2, rows, rows), F32),
            pltpu.VMEM(whole, BF16),
            pltpu.VMEM(whole, BF16),
            pltpu.SemaphoreType.DMA((len(parts),)),
        ],
        compiler_params=pltpu.CompilerParams(vmem_limit_bytes=24 * 1024 * 1024),
        cost_estimate=pl.CostEstimate(flops=16 * features**3, bytes_accessed=2**22, transcendentals=0),
        name="polar",
    )(place, *parts)


def rotate_kernel(rows, factor, out, held, product, in_sems, out_sems):
    block = held.shape[1]
    parts = range(held.shape[0])

    def fetch(k):
        return pltpu.make_async_copy(rows.at[pl.ds(k * block, block), :], held.at[k], in_sems.at[k])

    def store(k):
        return pltpu.make_async_copy(product.at[k], out.at[pl.ds(k * block, block), :], out_sems.at[k])

    for k in parts:
        fetch(k).start()
    for k in parts:
        fetch(k).wait()
        product[k] = jnp.dot(held[k], factor[...], preferred_element_type=F32)
        store(k).start()
    for k in parts:
        store(k).wait()


def rotate(rows, factor):
    count, features = rows.shape
    parts = 4
    block = count // parts
    return pl.pallas_call(
        rotate_kernel,
        out_shape=jax.ShapeDtypeStruct((count, features), F32),
        in_specs=[pl.BlockSpec(memory_space=pltpu.HBM), pl.BlockSpec(memory_space=pltpu.VMEM)],
        out_specs=pl.BlockSpec(memory_space=pltpu.HBM),
        scratch_shapes=[
            pltpu.VMEM((parts, block, features), BF16),
            pltpu.VMEM((parts, block, features), F32),
            pltpu.SemaphoreType.DMA((parts,)),
            pltpu.SemaphoreType.DMA((parts,)),
        ],
        compiler_params=pltpu.CompilerParams(vmem_limit_bytes=12 * 1024 * 1024),
        cost_estimate=pl.CostEstimate(
            flops=2 * count * features**2, bytes_accessed=5 * 2**20, transcendentals=0
        ),
        name="rotate",
    )(rows, factor)


def local(old_rows, new_rows, list_ids, owner_map):
    features = old_rows.shape[1]
    members = lax.axis_size(MEM)
    place = jnp.stack([lax.axis_index("yl"), lax.axis_index("core"), lax.axis_index(MEM)])
    sent = outgoing_rows(old_rows, list_ids, owner_map, members)
    mine = covariance_slabs(old_rows, new_rows)
    mine, sent = lax.optimization_barrier((mine, sent))
    received = exchange(sent, MEM)
    rows = mine.shape[0] // 2
    up = [(i, (i + 1) % WIDTH) for i in range(WIDTH)]
    down = [(i, (i - 1) % WIDTH) for i in range(WIDTH)]
    parts = [mine, lax.ppermute(mine[:rows], Y, up), lax.ppermute(mine[rows:], Y, down)]
    parts += [swap_core(part) for part in parts]
    parts = [pltpu.with_memory_space_constraint(part, pltpu.HBM) for part in parts]
    factor, own_rows = polar(place.astype(jnp.int32), parts, features // members)
    received = pltpu.with_memory_space_constraint(received, pltpu.HBM)
    return (rotate(received, factor), own_rows)


def solution(mesh):
    shape = mesh.shape
    grid = mesh.devices.reshape(2, WIDTH // 2, 2, 4, shape["mem"] // 8, 2)
    fine = Mesh(grid, ALL)
    in_specs = (P(ALL, None), P(ALL, None), P(ALL), P())
    out_specs = (P(ALL, None), P(MEM, None))
    return jax.shard_map(local, mesh=fine, in_specs=in_specs, out_specs=out_specs, check_vma=False)
```

```python
import math

import jax
import jax.numpy as jnp
from jax import lax
from jax.experimental import pallas as pl
from jax.experimental.pallas import tpu as pltpu
from jax.sharding import Mesh
from jax.sharding import PartitionSpec as P

WIDTH = 4

EPSILON = 1e-06
COEFF_ONE = 3.4445
COEFF_THREE = -4.775
COEFF_FIVE = 2.0315

ALL = ("y", "core", "x", "zh", "zl")
MEM = ("x", "zh", "zl")
SPREAD = ("y", "x", "zl")
Z = ("zh", "zl")
F32 = jnp.float32
BF16 = jnp.bfloat16


def dot(a, b):
    return jnp.dot(a, b, preferred_element_type=F32)


def swap_core(value):
    return lax.ppermute(value, "core", [(0, 1), (1, 0)])


def exchange(value, axes):
    return lax.all_to_all(value, axes, split_axis=0, concat_axis=0, tiled=True)


def outgoing_rows(old_rows, list_ids, owner_map, members):
    row_total = old_rows.shape[0]
    capacity = 2 * row_total // members
    owner = owner_map[list_ids]
    index = jnp.arange(row_total, dtype=jnp.int32)
    earlier = (owner[:, None] == owner[None, :]) & (index[None, :] < index[:, None])
    target = owner * capacity + jnp.sum(earlier.astype(jnp.int32), axis=1)
    slots = jnp.arange(members * capacity, dtype=jnp.int32)
    place = (slots[:, None] == target[None, :]).astype(BF16)
    return dot(place, old_rows).astype(BF16)


def sum_kernel(terms, out):
    total = terms[0].astype(F32)
    for k in range(1, terms.shape[0]):
        total += terms[k].astype(F32)
    for k in range(out.shape[0]):
        out[k] = total.astype(BF16)


def sum_and_copy(terms, copies):
    _, rows, columns = terms.shape
    vmem = pl.BlockSpec(memory_space=pltpu.VMEM)
    return pl.pallas_call(
        sum_kernel,
        out_shape=jax.ShapeDtypeStruct((copies, rows, columns), BF16),
        in_specs=[vmem],
        out_specs=vmem,
        compiler_params=pltpu.CompilerParams(vmem_limit_bytes=8 * 1024 * 1024),
        cost_estimate=pl.CostEstimate(flops=terms.size, bytes_accessed=2**20, transcendentals=0),
        name="sum_and_copy",
    )(terms)


def sum_pair_kernel(terms, out):
    rows = terms.shape[1]
    for low in range(2):
        total = terms[low].astype(F32)
        for k in range(low + 2, terms.shape[0], 2):
            total += terms[k].astype(F32)
        out[low * rows : (low + 1) * rows, :] = total.astype(BF16)


def sum_pairs(terms):
    _, rows, columns = terms.shape
    vmem = pl.BlockSpec(memory_space=pltpu.VMEM)
    return pl.pallas_call(
        sum_pair_kernel,
        out_shape=jax.ShapeDtypeStruct((2 * rows, columns), BF16),
        in_specs=[vmem],
        out_specs=vmem,
        compiler_params=pltpu.CompilerParams(vmem_limit_bytes=8 * 1024 * 1024),
        cost_estimate=pl.CostEstimate(flops=terms.size, bytes_accessed=2**19, transcendentals=0),
        name="sum_pairs",
    )(terms)


def covariance_block(old_rows, new_rows):
    features = old_rows.shape[1]
    half = features // 2
    core = lax.axis_index("core")
    mine = lax.dynamic_slice_in_dim(new_rows, core * half, half, 1)
    theirs = lax.dynamic_slice_in_dim(new_rows, (1 - core) * half, half, 1)
    old_pair = swap_core(old_rows)
    new_pair = swap_core(theirs)
    part = (dot(old_rows.T, mine) + dot(old_pair.T, new_pair)).astype(BF16)
    planes = lax.axis_size(SPREAD)
    depth = lax.axis_size(Z)
    block = features // planes
    arrived = exchange(part, SPREAD).reshape(planes, block, half)
    copies = sum_and_copy(arrived, depth)
    return sum_pairs(exchange(copies, Z).reshape(depth, block, half))


def gather_shifts(value, axis):
    steps = {s: [(i, (i + s) % WIDTH) for i in range(WIDTH)] for s in range(1, WIDTH)}
    return [value] + [lax.ppermute(value, axis, steps[s]) for s in range(1, WIDTH)]


def polar_kernel(place, *refs):
    owns, others = refs[0:WIDTH], refs[WIDTH : 2 * WIDTH]
    result, rotation = refs[2 * WIDTH : 2 * WIDTH + 2]
    start, middle, gram32, gram, poly, slab_sem = refs[2 * WIDTH + 2 :]
    rows, half = owns[0].shape
    features = 2 * half
    span = [slice(s * rows, (s + 1) * rows) for s in range(WIDTH)]
    pairs = [(s, t) for s in range(WIDTH) for t in range(s, WIDTH)]

    def product(a, b):
        return lax.dot_general(a, b, (((1,), (1,)), ((), ())), preferred_element_type=F32)

    def mirrored(target, s, t, value):
        target[span[s], span[t]] = value.astype(BF16)
        if s != t:
            target[span[t], span[s]] = value.T.astype(BF16)

    own_slab = pltpu.make_async_copy(owns[0], start.at[span[0], pl.ds(0, half)], slab_sem)
    own_slab.start()
    for s in range(WIDTH):
        if s:
            start[span[s], :half] = owns[s][...]
        start[span[s], half:] = others[s][...]
    own_slab.wait()
    squares = jnp.zeros((1, 1), F32)
    diagonal = lax.broadcasted_iota(jnp.int32, (rows, rows), 0) == lax.broadcasted_iota(
        jnp.int32, (rows, rows), 1
    )
    for k, (s, t) in enumerate(pairs):
        value = product(start[span[s], :], start[span[t], :])
        gram32[k] = value
        if s == t:
            squares += jnp.sum(jnp.where(diagonal, value, 0.0), keepdims=True)
    scale = 0.25 * math.sqrt(features) / jnp.sqrt(squares + EPSILON)
    for k, (s, t) in enumerate(pairs):
        mirrored(gram, s, t, gram32[k] * (scale * scale))

    def polynomial():
        for s, t in pairs:
            square = product(gram[span[s], :], gram[span[t], :])
            mirrored(poly, s, t, COEFF_THREE * gram[span[s], span[t]].astype(F32) + COEFF_FIVE * square)

    def advance(source, s):
        moved = jnp.dot(poly[span[s], :], source[...], preferred_element_type=F32)
        return COEFF_ONE * source[span[s], :].astype(F32) + moved

    polynomial()
    for s in range(WIDTH):
        middle[span[s], :] = (advance(start, s) * scale).astype(BF16)
    for s, t in pairs:
        mirrored(gram, s, t, product(middle[span[s], :], middle[span[t], :]))
    polynomial()
    y, core, member, x = place[0], place[1], place[2], place[3]
    block = rows // WIDTH
    sides = [pl.ds(pl.multiple_of(side * half, half), half) for side in (core, 1 - core)]
    for s in range(WIDTH):
        value = advance(middle, s).astype(BF16)
        for j in range(WIDTH):
            first = lax.rem(y - s + WIDTH, WIDTH) * rows + lax.rem(x - j + WIDTH, WIDTH) * block
            held = value[j * block : (j + 1) * block]
            result[pl.ds(pl.multiple_of(first, block), block), sides[0]] = held[:, :half]
            result[pl.ds(pl.multiple_of(first, block), block), sides[1]] = held[:, half:]
    kept = rotation.shape[0]
    rotation[...] = result[pl.ds(pl.multiple_of(member * kept, kept), kept), :]


def polar(place, owns, others, block_rows):
    rows, half = owns[0].shape
    features = 2 * half
    whole = (features, features)

    vmem = pl.BlockSpec(memory_space=pltpu.VMEM)
    return pl.pallas_call(
        polar_kernel,
        out_shape=(
            jax.ShapeDtypeStruct(whole, BF16),
            jax.ShapeDtypeStruct((block_rows, features), BF16),
        ),
        in_specs=[pl.BlockSpec(memory_space=pltpu.SMEM), pl.BlockSpec(memory_space=pl.ANY)]
        + [vmem] * (2 * WIDTH - 1),
        out_specs=(vmem, vmem),
        scratch_shapes=[
            pltpu.VMEM(whole, BF16),
            pltpu.VMEM(whole, BF16),
            pltpu.VMEM((WIDTH * (WIDTH + 1) // 2, rows, rows), F32),
            pltpu.VMEM(whole, BF16),
            pltpu.VMEM(whole, BF16),
            pltpu.SemaphoreType.DMA,
        ],
        compiler_params=pltpu.CompilerParams(vmem_limit_bytes=24 * 1024 * 1024),
        cost_estimate=pl.CostEstimate(flops=9 * features**3, bytes_accessed=2**22, transcendentals=0),
        name="polar",
    )(place, *owns, *others)


def rotate_kernel(rows, factor, out, held, product, in_sems, out_sems):
    block = held.shape[1]
    parts = range(held.shape[0])

    def fetch(k):
        return pltpu.make_async_copy(rows.at[pl.ds(k * block, block), :], held.at[k], in_sems.at[k])

    def store(k):
        return pltpu.make_async_copy(product.at[k], out.at[pl.ds(k * block, block), :], out_sems.at[k])

    for k in parts:
        fetch(k).start()
    for k in parts:
        fetch(k).wait()
        product[k] = jnp.dot(held[k], factor[...], preferred_element_type=F32)
        store(k).start()
    for k in parts:
        store(k).wait()


def rotate(rows, factor):
    count, features = rows.shape
    parts = 4
    block = count // parts
    return pl.pallas_call(
        rotate_kernel,
        out_shape=jax.ShapeDtypeStruct((count, features), F32),
        in_specs=[pl.BlockSpec(memory_space=pltpu.HBM), pl.BlockSpec(memory_space=pltpu.VMEM)],
        out_specs=pl.BlockSpec(memory_space=pltpu.HBM),
        scratch_shapes=[
            pltpu.VMEM((parts, block, features), BF16),
            pltpu.VMEM((parts, block, features), F32),
            pltpu.SemaphoreType.DMA((parts,)),
            pltpu.SemaphoreType.DMA((parts,)),
        ],
        compiler_params=pltpu.CompilerParams(vmem_limit_bytes=12 * 1024 * 1024),
        cost_estimate=pl.CostEstimate(
            flops=2 * count * features**2, bytes_accessed=5 * 2**20, transcendentals=0
        ),
        name="rotate",
    )(rows, factor)


def local(old_rows, new_rows, list_ids, owner_map):
    features = old_rows.shape[1]
    members = lax.axis_size(MEM)
    place = jnp.stack([lax.axis_index(axis) for axis in ("y", "core", MEM, "x")]).astype(jnp.int32)
    sent = outgoing_rows(old_rows, list_ids, owner_map, members)
    block = covariance_block(old_rows, new_rows)
    block, sent = lax.optimization_barrier((block, sent))
    received = exchange(sent, MEM)
    slab = jnp.concatenate(gather_shifts(block, "x"), axis=0)
    owns = gather_shifts(slab, "y")
    others = [swap_core(own) for own in owns]
    factor, own_rows = polar(place, owns, others, features // members)
    return (rotate(received, factor), own_rows)


def solution(mesh):
    shape = mesh.shape
    grid = mesh.devices.reshape(WIDTH, 2, 4, shape["mem"] // 8, 2)
    fine = Mesh(grid, ALL)
    in_specs = (P(ALL, None), P(ALL, None), P(ALL), P())
    out_specs = (P(ALL, None), P(MEM, None))
    return jax.shard_map(local, mesh=fine, in_specs=in_specs, out_specs=out_specs, check_vma=False)
```

```python
import math

import jax
import jax.numpy as jnp
from jax import lax
from jax.experimental import pallas as pl
from jax.experimental.pallas import tpu as pltpu
from jax.sharding import Mesh
from jax.sharding import PartitionSpec as P

WIDTH = 4

EPSILON = 1e-06
COEFF_ONE = 3.4445
COEFF_THREE = -4.775
COEFF_FIVE = 2.0315

ALL = ("y", "core", "x", "zh", "zl")
MEM = ("x", "zh", "zl")
SPREAD = ("y", "x", "zl")
Z = ("zh", "zl")
F32 = jnp.float32
BF16 = jnp.bfloat16


def dot(a, b):
    return jnp.dot(a, b, preferred_element_type=F32)


def swap_core(value):
    return lax.ppermute(value, "core", [(0, 1), (1, 0)])


def exchange(value, axes):
    return lax.all_to_all(value, axes, split_axis=0, concat_axis=0, tiled=True)


def outgoing_rows(old_rows, list_ids, owner_map, members):
    row_total = old_rows.shape[0]
    capacity = 2 * row_total // members
    owner = owner_map[list_ids]
    index = jnp.arange(row_total, dtype=jnp.int32)
    earlier = (owner[:, None] == owner[None, :]) & (index[None, :] < index[:, None])
    target = owner * capacity + jnp.sum(earlier.astype(jnp.int32), axis=1)
    slots = jnp.arange(members * capacity, dtype=jnp.int32)
    place = (slots[:, None] == target[None, :]).astype(BF16)
    return dot(place, old_rows).astype(BF16)


def sum_kernel(terms, out):
    total = terms[0].astype(F32)
    for k in range(1, terms.shape[0]):
        total += terms[k].astype(F32)
    for k in range(out.shape[0]):
        out[k] = total.astype(BF16)


def sum_and_copy(terms, copies):
    _, rows, columns = terms.shape
    vmem = pl.BlockSpec(memory_space=pltpu.VMEM)
    return pl.pallas_call(
        sum_kernel,
        out_shape=jax.ShapeDtypeStruct((copies, rows, columns), BF16),
        in_specs=[vmem],
        out_specs=vmem,
        compiler_params=pltpu.CompilerParams(vmem_limit_bytes=8 * 1024 * 1024),
        cost_estimate=pl.CostEstimate(flops=terms.size, bytes_accessed=2**20, transcendentals=0),
        name="sum_and_copy",
    )(terms)


def sum_pair_kernel(terms, out):
    rows = terms.shape[1]
    for low in range(2):
        total = terms[low].astype(F32)
        for k in range(low + 2, terms.shape[0], 2):
            total += terms[k].astype(F32)
        out[low * rows : (low + 1) * rows, :] = total.astype(BF16)


def sum_pairs(terms):
    _, rows, columns = terms.shape
    vmem = pl.BlockSpec(memory_space=pltpu.VMEM)
    return pl.pallas_call(
        sum_pair_kernel,
        out_shape=jax.ShapeDtypeStruct((2 * rows, columns), BF16),
        in_specs=[vmem],
        out_specs=vmem,
        compiler_params=pltpu.CompilerParams(vmem_limit_bytes=8 * 1024 * 1024),
        cost_estimate=pl.CostEstimate(flops=terms.size, bytes_accessed=2**19, transcendentals=0),
        name="sum_pairs",
    )(terms)


def covariance_block(old_rows, new_rows):
    features = old_rows.shape[1]
    half = features // 2
    core = lax.axis_index("core")
    mine = lax.dynamic_slice_in_dim(new_rows, core * half, half, 1)
    theirs = lax.dynamic_slice_in_dim(new_rows, (1 - core) * half, half, 1)
    old_pair = swap_core(old_rows)
    new_pair = swap_core(theirs)
    part = (dot(old_rows.T, mine) + dot(old_pair.T, new_pair)).astype(BF16)
    planes = lax.axis_size(SPREAD)
    depth = lax.axis_size(Z)
    block = features // planes
    arrived = exchange(part, SPREAD).reshape(planes, block, half)
    copies = sum_and_copy(arrived, depth)
    return sum_pairs(exchange(copies, Z).reshape(depth, block, half))


def gather_shifts(value, axis):
    steps = {s: [(i, (i + s) % WIDTH) for i in range(WIDTH)] for s in range(1, WIDTH)}
    return [value] + [lax.ppermute(value, axis, steps[s]) for s in range(1, WIDTH)]


def polar_kernel(place, *refs):
    owns, others = refs[0:WIDTH], refs[WIDTH : 2 * WIDTH]
    result, rotation = refs[2 * WIDTH : 2 * WIDTH + 2]
    start, middle, gram32, gram, poly, slab_sem = refs[2 * WIDTH + 2 :]
    rows, half = owns[0].shape
    features = 2 * half
    span = [slice(s * rows, (s + 1) * rows) for s in range(WIDTH)]
    pairs = [(s, t) for s in range(WIDTH) for t in range(s, WIDTH)]

    def product(a, b):
        return lax.dot_general(a, b, (((1,), (1,)), ((), ())), preferred_element_type=F32)

    def mirrored(target, s, t, value):
        target[span[s], span[t]] = value.astype(BF16)
        if s != t:
            target[span[t], span[s]] = value.T.astype(BF16)

    own_slab = pltpu.make_async_copy(owns[0], start.at[span[0], pl.ds(0, half)], slab_sem)
    own_slab.start()
    for s in range(WIDTH):
        if s:
            start[span[s], :half] = owns[s][...]
        start[span[s], half:] = others[s][...]
    own_slab.wait()
    squares = jnp.zeros((1, 1), F32)
    diagonal = lax.broadcasted_iota(jnp.int32, (rows, rows), 0) == lax.broadcasted_iota(
        jnp.int32, (rows, rows), 1
    )
    for k, (s, t) in enumerate(pairs):
        value = product(start[span[s], :], start[span[t], :])
        gram32[k] = value
        if s == t:
            squares += jnp.sum(jnp.where(diagonal, value, 0.0), keepdims=True)
    scale = 0.25 * math.sqrt(features) / jnp.sqrt(squares + EPSILON)
    for k, (s, t) in enumerate(pairs):
        mirrored(gram, s, t, gram32[k] * (scale * scale))

    def polynomial():
        for s, t in pairs:
            square = product(gram[span[s], :], gram[span[t], :])
            mirrored(poly, s, t, COEFF_THREE * gram[span[s], span[t]].astype(F32) + COEFF_FIVE * square)

    def advance(source, s):
        moved = jnp.dot(poly[span[s], :], source[...], preferred_element_type=F32)
        return COEFF_ONE * source[span[s], :].astype(F32) + moved

    polynomial()
    for s in range(WIDTH):
        middle[span[s], :] = (advance(start, s) * scale).astype(BF16)
    for s, t in pairs:
        mirrored(gram, s, t, product(middle[span[s], :], middle[span[t], :]))
    polynomial()
    y, core, member, x = place[0], place[1], place[2], place[3]
    block = rows // WIDTH
    sides = [pl.ds(pl.multiple_of(side * half, half), half) for side in (core, 1 - core)]
    for s in range(WIDTH):
        value = advance(middle, s).astype(BF16)
        for j in range(WIDTH):
            first = lax.rem(y - s + WIDTH, WIDTH) * rows + lax.rem(x - j + WIDTH, WIDTH) * block
            held = value[j * block : (j + 1) * block]
            result[pl.ds(pl.multiple_of(first, block), block), sides[0]] = held[:, :half]
            result[pl.ds(pl.multiple_of(first, block), block), sides[1]] = held[:, half:]
    kept = rotation.shape[0]
    rotation[...] = result[pl.ds(pl.multiple_of(member * kept, kept), kept), :]


def polar(place, owns, others, block_rows):
    rows, half = owns[0].shape
    features = 2 * half
    whole = (features, features)

    vmem = pl.BlockSpec(memory_space=pltpu.VMEM)
    return pl.pallas_call(
        polar_kernel,
        out_shape=(
            jax.ShapeDtypeStruct(whole, BF16),
            jax.ShapeDtypeStruct((block_rows, features), BF16),
        ),
        in_specs=[pl.BlockSpec(memory_space=pltpu.SMEM), pl.BlockSpec(memory_space=pl.ANY)]
        + [vmem] * (2 * WIDTH - 1),
        out_specs=(vmem, vmem),
        scratch_shapes=[
            pltpu.VMEM(whole, BF16),
            pltpu.VMEM(whole, BF16),
            pltpu.VMEM((WIDTH * (WIDTH + 1) // 2, rows, rows), F32),
            pltpu.VMEM(whole, BF16),
            pltpu.VMEM(whole, BF16),
            pltpu.SemaphoreType.DMA,
        ],
        compiler_params=pltpu.CompilerParams(vmem_limit_bytes=24 * 1024 * 1024),
        cost_estimate=pl.CostEstimate(flops=13 * features**3, bytes_accessed=2**22, transcendentals=0),
        name="polar",
    )(place, *owns, *others)


def rotate_kernel(rows, factor, out, held, product, in_sems, out_sems):
    block = held.shape[1]
    parts = range(held.shape[0])

    def fetch(k):
        return pltpu.make_async_copy(rows.at[pl.ds(k * block, block), :], held.at[k], in_sems.at[k])

    def store(k):
        return pltpu.make_async_copy(product.at[k], out.at[pl.ds(k * block, block), :], out_sems.at[k])

    for k in parts:
        fetch(k).start()
    for k in parts:
        fetch(k).wait()
        product[k] = jnp.dot(held[k], factor[...], preferred_element_type=F32)
        store(k).start()
    for k in parts:
        store(k).wait()


def rotate(rows, factor):
    count, features = rows.shape
    parts = 4
    block = count // parts
    return pl.pallas_call(
        rotate_kernel,
        out_shape=jax.ShapeDtypeStruct((count, features), F32),
        in_specs=[pl.BlockSpec(memory_space=pltpu.HBM), pl.BlockSpec(memory_space=pltpu.VMEM)],
        out_specs=pl.BlockSpec(memory_space=pltpu.HBM),
        scratch_shapes=[
            pltpu.VMEM((parts, block, features), BF16),
            pltpu.VMEM((parts, block, features), F32),
            pltpu.SemaphoreType.DMA((parts,)),
            pltpu.SemaphoreType.DMA((parts,)),
        ],
        compiler_params=pltpu.CompilerParams(vmem_limit_bytes=12 * 1024 * 1024),
        cost_estimate=pl.CostEstimate(
            flops=2 * count * features**2, bytes_accessed=5 * 2**20, transcendentals=0
        ),
        name="rotate",
    )(rows, factor)


def local(old_rows, new_rows, list_ids, owner_map):
    features = old_rows.shape[1]
    members = lax.axis_size(MEM)
    place = jnp.stack([lax.axis_index(axis) for axis in ("y", "core", MEM, "x")]).astype(jnp.int32)
    sent = outgoing_rows(old_rows, list_ids, owner_map, members)
    block = covariance_block(old_rows, new_rows)
    block, sent = lax.optimization_barrier((block, sent))
    received = exchange(sent, MEM)
    slab = jnp.concatenate(gather_shifts(block, "x"), axis=0)
    owns = gather_shifts(slab, "y")
    others = [swap_core(own) for own in owns]
    factor, own_rows = polar(place, owns, others, features // members)
    return (rotate(received, factor), own_rows)


def solution(mesh):
    shape = mesh.shape
    grid = mesh.devices.reshape(WIDTH, 2, 4, shape["mem"] // 8, 2)
    fine = Mesh(grid, ALL)
    in_specs = (P(ALL, None), P(ALL, None), P(ALL), P())
    out_specs = (P(ALL, None), P(MEM, None))
    return jax.shard_map(local, mesh=fine, in_specs=in_specs, out_specs=out_specs, check_vma=False)
```

```python
import math

import jax
import jax.numpy as jnp
from jax import lax
from jax.experimental import pallas as pl
from jax.experimental.pallas import tpu as pltpu
from jax.sharding import Mesh
from jax.sharding import PartitionSpec as P

WIDTH = 4

EPSILON = 1e-06
COEFF_ONE = 3.4445
COEFF_THREE = -4.775
COEFF_FIVE = 2.0315

ALL = ("y", "core", "x", "zh", "zl")
MEM = ("x", "zh", "zl")
SPREAD = ("y", "x", "zl")
Z = ("zh", "zl")
F32 = jnp.float32
BF16 = jnp.bfloat16


def dot(a, b):
    return jnp.dot(a, b, preferred_element_type=F32)


def swap_core(value):
    return lax.ppermute(value, "core", [(0, 1), (1, 0)])


def exchange(value, axes):
    return lax.all_to_all(value, axes, split_axis=0, concat_axis=0, tiled=True)


def outgoing_rows(old_rows, list_ids, owner_map, members):
    row_total = old_rows.shape[0]
    capacity = 2 * row_total // members
    owner = owner_map[list_ids]
    index = jnp.arange(row_total, dtype=jnp.int32)
    earlier = (owner[:, None] == owner[None, :]) & (index[None, :] < index[:, None])
    target = owner * capacity + jnp.sum(earlier.astype(jnp.int32), axis=1)
    slots = jnp.arange(members * capacity, dtype=jnp.int32)
    place = (slots[:, None] == target[None, :]).astype(BF16)
    return dot(place, old_rows).astype(BF16)


def sum_kernel(terms, out):
    total = terms[0].astype(F32)
    for k in range(1, terms.shape[0]):
        total += terms[k].astype(F32)
    for k in range(out.shape[0]):
        out[k] = total.astype(BF16)


def sum_and_copy(terms, copies):
    _, rows, columns = terms.shape
    vmem = pl.BlockSpec(memory_space=pltpu.VMEM)
    return pl.pallas_call(
        sum_kernel,
        out_shape=jax.ShapeDtypeStruct((copies, rows, columns), BF16),
        in_specs=[vmem],
        out_specs=vmem,
        compiler_params=pltpu.CompilerParams(vmem_limit_bytes=8 * 1024 * 1024),
        cost_estimate=pl.CostEstimate(flops=terms.size, bytes_accessed=2**20, transcendentals=0),
        name="sum_and_copy",
    )(terms)


def sum_pair_kernel(terms, out):
    rows = terms.shape[1]
    for low in range(2):
        total = terms[low].astype(F32)
        for k in range(low + 2, terms.shape[0], 2):
            total += terms[k].astype(F32)
        out[low * rows : (low + 1) * rows, :] = total.astype(BF16)


def sum_pairs(terms):
    _, rows, columns = terms.shape
    vmem = pl.BlockSpec(memory_space=pltpu.VMEM)
    return pl.pallas_call(
        sum_pair_kernel,
        out_shape=jax.ShapeDtypeStruct((2 * rows, columns), BF16),
        in_specs=[vmem],
        out_specs=vmem,
        compiler_params=pltpu.CompilerParams(vmem_limit_bytes=8 * 1024 * 1024),
        cost_estimate=pl.CostEstimate(flops=terms.size, bytes_accessed=2**19, transcendentals=0),
        name="sum_pairs",
    )(terms)


def covariance_block(old_rows, new_rows):
    features = old_rows.shape[1]
    half = features // 2
    core = lax.axis_index("core")
    mine = lax.dynamic_slice_in_dim(new_rows, core * half, half, 1)
    theirs = lax.dynamic_slice_in_dim(new_rows, (1 - core) * half, half, 1)
    old_pair = swap_core(old_rows)
    new_pair = swap_core(theirs)
    part = (dot(old_rows.T, mine) + dot(old_pair.T, new_pair)).astype(BF16)
    planes = lax.axis_size(SPREAD)
    depth = lax.axis_size(Z)
    block = features // planes
    arrived = exchange(part, SPREAD).reshape(planes, block, half)
    copies = sum_and_copy(arrived, depth)
    return sum_pairs(exchange(copies, Z).reshape(depth, block, half))


def gather_shifts(value, axis):
    steps = {s: [(i, (i + s) % WIDTH) for i in range(WIDTH)] for s in range(1, WIDTH)}
    return [value] + [lax.ppermute(value, axis, steps[s]) for s in range(1, WIDTH)]


def polar_kernel(place, *refs):
    owns, others = refs[0:WIDTH], refs[WIDTH : 2 * WIDTH]
    result, rotation = refs[2 * WIDTH : 2 * WIDTH + 2]
    start, middle, gram32, gram, poly, slab_sem, out_sems = refs[2 * WIDTH + 2 :]
    rows, half = owns[0].shape
    features = 2 * half
    span = [slice(s * rows, (s + 1) * rows) for s in range(WIDTH)]
    pairs = [(s, t) for s in range(WIDTH) for t in range(s, WIDTH)]

    def product(a, b):
        return lax.dot_general(a, b, (((1,), (1,)), ((), ())), preferred_element_type=F32)

    def mirrored(target, s, t, value):
        target[span[s], span[t]] = value.astype(BF16)
        if s != t:
            target[span[t], span[s]] = value.T.astype(BF16)

    own_slab = pltpu.make_async_copy(owns[0], start.at[span[0], pl.ds(0, half)], slab_sem)
    own_slab.start()
    for s in range(WIDTH):
        if s:
            start[span[s], :half] = owns[s][...]
        start[span[s], half:] = others[s][...]
    own_slab.wait()
    squares = jnp.zeros((1, 1), F32)
    diagonal = lax.broadcasted_iota(jnp.int32, (rows, rows), 0) == lax.broadcasted_iota(
        jnp.int32, (rows, rows), 1
    )
    for k, (s, t) in enumerate(pairs):
        value = product(start[span[s], :], start[span[t], :])
        gram32[k] = value
        if s == t:
            squares += jnp.sum(jnp.where(diagonal, value, 0.0), keepdims=True)
    scale = 0.25 * math.sqrt(features) / jnp.sqrt(squares + EPSILON)
    for k, (s, t) in enumerate(pairs):
        mirrored(gram, s, t, gram32[k] * (scale * scale))

    def polynomial():
        for s, t in pairs:
            square = product(gram[span[s], :], gram[span[t], :])
            mirrored(poly, s, t, COEFF_THREE * gram[span[s], span[t]].astype(F32) + COEFF_FIVE * square)

    def advance(source, s):
        moved = jnp.dot(poly[span[s], :], source[...], preferred_element_type=F32)
        return COEFF_ONE * source[span[s], :].astype(F32) + moved

    polynomial()
    for s in range(WIDTH):
        middle[span[s], :] = (advance(start, s) * scale).astype(BF16)
    for s, t in pairs:
        mirrored(gram, s, t, product(middle[span[s], :], middle[span[t], :]))
    polynomial()
    y, core, member, x = place[0], place[1], place[2], place[3]
    block = rows // WIDTH
    sides = [pl.ds(pl.multiple_of(side * half, half), half) for side in (core, 1 - core)]
    stores = []
    for s in range(WIDTH):
        value = advance(middle, s).astype(BF16)
        base = lax.rem(y - s + WIDTH, WIDTH) * rows
        for j in range(WIDTH):
            first = base + lax.rem(x - j + WIDTH, WIDTH) * block
            held = value[j * block : (j + 1) * block]
            start[pl.ds(pl.multiple_of(first, block), block), sides[0]] = held[:, :half]
            start[pl.ds(pl.multiple_of(first, block), block), sides[1]] = held[:, half:]
        slab = pl.ds(pl.multiple_of(base, rows), rows)
        stores.append(pltpu.make_async_copy(start.at[slab, :], result.at[slab, :], out_sems.at[s]))
        stores[s].start()
    kept = rotation.shape[0]
    rotation[...] = start[pl.ds(pl.multiple_of(member * kept, kept), kept), :]
    for store in stores:
        store.wait()


def polar(place, owns, others, block_rows):
    rows, half = owns[0].shape
    features = 2 * half
    whole = (features, features)

    vmem = pl.BlockSpec(memory_space=pltpu.VMEM)
    return pl.pallas_call(
        polar_kernel,
        out_shape=(
            pltpu.HBM(whole, BF16),
            jax.ShapeDtypeStruct((block_rows, features), BF16),
        ),
        in_specs=[pl.BlockSpec(memory_space=pltpu.SMEM), pl.BlockSpec(memory_space=pl.ANY)]
        + [vmem] * (2 * WIDTH - 1),
        out_specs=(pl.BlockSpec(memory_space=pl.ANY), vmem),
        scratch_shapes=[
            pltpu.VMEM(whole, BF16),
            pltpu.VMEM(whole, BF16),
            pltpu.VMEM((WIDTH * (WIDTH + 1) // 2, rows, rows), F32),
            pltpu.VMEM(whole, BF16),
            pltpu.VMEM(whole, BF16),
            pltpu.SemaphoreType.DMA,
            pltpu.SemaphoreType.DMA((WIDTH,)),
        ],
        compiler_params=pltpu.CompilerParams(vmem_limit_bytes=24 * 1024 * 1024),
        cost_estimate=pl.CostEstimate(flops=13 * features**3, bytes_accessed=2**22, transcendentals=0),
        name="polar",
    )(place, *owns, *others)


def rotate_kernel(rows, factor, out, weights, product, in_sems, out_sems):
    block = rows.shape[1] // in_sems.shape[0]
    parts = range(in_sems.shape[0])
    columns = [pl.ds(k * block, block) for k in parts]

    def fetch(k):
        return pltpu.make_async_copy(factor.at[:, columns[k]], weights.at[:, columns[k]], in_sems.at[k])

    def store(k):
        return pltpu.make_async_copy(product.at[:, columns[k]], out.at[:, columns[k]], out_sems.at[k])

    for k in parts:
        fetch(k).start()
    for k in parts:
        fetch(k).wait()
        product[:, columns[k]] = jnp.dot(rows[...], weights[:, columns[k]], preferred_element_type=F32)
        store(k).start()
    for k in parts:
        store(k).wait()


def rotate(rows, factor):
    count, features = rows.shape
    parts = 4
    anywhere = pl.BlockSpec(memory_space=pl.ANY)
    return pl.pallas_call(
        rotate_kernel,
        out_shape=jax.ShapeDtypeStruct((count, features), F32),
        in_specs=[pl.BlockSpec(memory_space=pltpu.VMEM), anywhere],
        out_specs=anywhere,
        scratch_shapes=[
            pltpu.VMEM((features, features), BF16),
            pltpu.VMEM((count, features), F32),
            pltpu.SemaphoreType.DMA((parts,)),
            pltpu.SemaphoreType.DMA((parts,)),
        ],
        compiler_params=pltpu.CompilerParams(vmem_limit_bytes=12 * 1024 * 1024),
        cost_estimate=pl.CostEstimate(
            flops=2 * count * features**2, bytes_accessed=5 * 2**20, transcendentals=0
        ),
        name="rotate",
    )(rows, factor)


def local(old_rows, new_rows, list_ids, owner_map):
    features = old_rows.shape[1]
    members = lax.axis_size(MEM)
    place = jnp.stack([lax.axis_index(axis) for axis in ("y", "core", MEM, "x")]).astype(jnp.int32)
    sent = outgoing_rows(old_rows, list_ids, owner_map, members)
    block = covariance_block(old_rows, new_rows)
    block, sent = lax.optimization_barrier((block, sent))
    received = exchange(sent, MEM)
    slab = jnp.concatenate(gather_shifts(block, "x"), axis=0)
    owns = gather_shifts(slab, "y")
    others = [swap_core(own) for own in owns]
    factor, own_rows = polar(place, owns, others, features // members)
    factor = pltpu.with_memory_space_constraint(factor, pltpu.HBM)
    return (rotate(received, factor), own_rows)


def solution(mesh):
    shape = mesh.shape
    grid = mesh.devices.reshape(WIDTH, 2, 4, shape["mem"] // 8, 2)
    fine = Mesh(grid, ALL)
    in_specs = (P(ALL, None), P(ALL, None), P(ALL), P())
    out_specs = (P(ALL, None), P(MEM, None))
    return jax.shard_map(local, mesh=fine, in_specs=in_specs, out_specs=out_specs, check_vma=False)
```
